512 devices in a mesh: ctx: 32 (over x, z), head: 16 (over y, core).
Axes of the slice: x: 4, y: 8, z: 8, core: 2. Of those that a mesh axis runs over, the one named last changes fastest.
Arguments:
- query: bfloat16 [8192, 6144], P('ctx', 'head'), may hold values from -6 to 6
- keys: bfloat16 [8192, 6144], P('ctx', 'head'), may hold values from -6 to 6
- values: bfloat16 [8192, 6144], P('ctx', 'head'), may hold values from -6 to 6
- span_slot: int32 [128], replicated, may hold values from 0 to 127, each once
- span_doc: int32 [128], replicated, may hold values from 0 to 3, never falling along the last dimension, each value on 1 to 64 neighbouring positions
- w_out: bfloat16 [6144, 6144], P('head', 'ctx'), may hold values from -0.078125 to 0.078125
Outputs:
- mixed: bfloat16 [8192, 6144], P(('ctx', 'head'))
The draws below stay inside these ranges and needn't reach their ends.
Inputs may be any that keep to these rules, and one draw needn't show every extreme that they name: `span_slot`: a permutation of the spans of the clip. `span_doc`: never falls along the clip; one sequence holds exactly 64 spans.
All inputs are finite; a program needn't handle non-finite values.
Results may differ from the reference program's by a relative error of at most 0.024.
Values may be sent and summed in bfloat16 or wider, within the bound.
A program may use at most 64 MiB of HBM per device.

```python
import math
import jax
import jax.numpy as jnp
import numpy as np
from jax import lax

HEADS = 48
HEAD_DIM = 128
D = 6144
SPAN = 64
TOKENS = 8192
NCHUNK = 128
N_HEAD = 16


def plant_pattern(key):
    sign_bits = jax.random.bernoulli(jax.random.fold_in(key, 101), 0.5, (HEADS * HEAD_DIM,))
    pattern = jnp.where(sign_bits, jnp.float32(1.0), jnp.float32(-1.0))
    chosen = jax.random.randint(jax.random.fold_in(key, 102), (NCHUNK,), 0, 4)
    strength = jnp.array([3.0, 4.0, 5.0, 6.0], jnp.float32)[chosen]
    return (pattern, strength)


def draw_query(key, part):
    pattern, strength = plant_pattern(key)
    key = jax.random.fold_in(key, 3)
    extent = (TOKENS, HEADS * HEAD_DIM)
    filler = jax.random.truncated_normal(key, -6.0, 6.0, extent, jnp.float32)
    within = jnp.arange(TOKENS, dtype=jnp.int32) % SPAN
    slot_index = jnp.arange(TOKENS, dtype=jnp.int32) // SPAN
    planted = strength[slot_index][:, None] * pattern[None, :]
    return jnp.where((within == 0)[:, None], planted, filler).astype(jnp.bfloat16)


def draw_keys(key, part):
    pattern, strength = plant_pattern(key)
    key = jax.random.fold_in(key, 5)
    extent = (TOKENS, HEADS * HEAD_DIM)
    filler = jax.random.truncated_normal(key, -6.0, 6.0, extent, jnp.float32)
    within = jnp.arange(TOKENS, dtype=jnp.int32) % SPAN
    first_rows = jnp.float32(3.5) * pattern[None, :]
    second_rows = jnp.float32(3.46875) * pattern[None, :]
    result = jnp.where((within == 0)[:, None], first_rows, filler)
    result = jnp.where((within == 1)[:, None], second_rows, result)
    return result.astype(jnp.bfloat16)


def block_scale(own_key, shape, shards, least, largest):
    loudness, own = 1.0, jax.random.fold_in(own_key, 6)
    for axis_at, blocks in shards:
        draws = jnp.exp(jax.random.uniform(jax.random.fold_in(own, axis_at), (blocks,), jnp.float32, least / len(shards), largest / len(shards)))
        loudness = loudness * jnp.repeat(draws, shape[axis_at] // blocks).reshape([-1 if axis == axis_at else 1 for axis in range(len(shape))])
    return loudness


def length_profile(number_of, total, reach, slope):
    portions = [(1 << 20) // math.isqrt(rank ** slope) + 1 for rank in range(2, number_of + 1)]
    surplus, given = total - reach - (number_of - 1), [1] * (number_of - 1)
    while surplus > 0:
        movable = [i for i in range(number_of - 1) if given[i] < reach]
        pool, budget = sum([portions[i] for i in movable]), surplus
        for i in movable:
            addition = min(reach - given[i], max(1, budget * portions[i] // pool), surplus)
            given[i] = given[i] + addition
            surplus = surplus - addition
    return np.array([reach] + given)


def uneven(own_key, amount, total, most, skew):
    if amount == 2:
        one = jax.random.randint(own_key, (), max(1, total - most), min(most, total - 1) + 1)
        return jnp.stack([one, total - one])
    sizes = jnp.asarray(length_profile(amount, total, most, skew), jnp.int32)
    twos = (amount - 1) // 2
    donor, receiver = sizes[1:1 + 2 * twos:2], sizes[2:2 + 2 * twos:2]
    slack = jnp.minimum(donor - 1, most - receiver)
    passed = jax.random.randint(jax.random.fold_in(own_key, 1), (twos,), 0, 1 << 20) % (slack + 1)
    sizes = sizes.at[1:1 + 2 * twos:2].set(donor - passed).at[2:2 + 2 * twos:2].set(receiver + passed)
    return sizes[jax.random.permutation(jax.random.fold_in(own_key, 2), amount)]


def bell_draw(rng, shape, width, limit, cuts=(), held_as=jnp.bfloat16):
    loudness = block_scale(rng, shape, cuts, -0.22, 0.18) if cuts else 1.0
    drawn = jax.random.normal(rng, shape, jnp.float32) * width * loudness
    return jnp.minimum(jnp.maximum(drawn, -limit), limit).astype(held_as)


def setup_inputs(seed: int = 0) -> dict:
    key_list = jax.random.split(jax.random.key(seed), 7)
    query = draw_query(jax.random.fold_in(key_list[6], 71), 0)
    keys = draw_keys(jax.random.fold_in(key_list[6], 71), 0)
    values = bell_draw(key_list[2], (TOKENS, HEADS * HEAD_DIM), 1.0, 6.0, ((0, 32), (1, 16)))
    span_slot = jax.random.permutation(key_list[3], NCHUNK).astype(jnp.int32)
    span_doc = jnp.searchsorted(jnp.cumsum(uneven(key_list[4], 4, NCHUNK, NCHUNK // 2, 1)), jnp.arange(NCHUNK), side="right").astype(jnp.int32)
    w_out = bell_draw(key_list[5], (HEADS * HEAD_DIM, D), (HEADS * HEAD_DIM) ** -0.5, 0.078125, ((0, 16), (1, 32)))
    return {"query": query, "keys": keys, "values": values, "span_slot": span_slot, "span_doc": span_doc, "w_out": w_out}


def reference(query, keys, values, span_slot, span_doc, w_out):
    slot_span = span_slot[(jnp.arange(TOKENS) // SPAN).astype(jnp.int32)]
    token_doc = span_doc[slot_span]
    block = min(512, TOKENS)
    blocks = TOKENS // block
    factor = HEAD_DIM ** -0.5

    def head_out(head):
        start_col = (head * HEAD_DIM).astype(jnp.int32)
        q_head = lax.dynamic_slice_in_dim(query, start_col, HEAD_DIM, 1)
        k_head = lax.dynamic_slice_in_dim(keys, start_col, HEAD_DIM, 1)
        v_head = lax.dynamic_slice_in_dim(values, start_col, HEAD_DIM, 1)

        def one_block(index):
            start = (index * block).astype(jnp.int32)
            q_rows = lax.dynamic_slice_in_dim(q_head, start, block, 0)
            q_span = lax.dynamic_slice_in_dim(slot_span, start, block, 0)
            q_doc = lax.dynamic_slice_in_dim(token_doc, start, block, 0)
            scores = jnp.dot(q_rows, k_head.T, preferred_element_type=jnp.float32) * factor
            visible = (q_doc[:, None] == token_doc[None, :]) & (slot_span[None, :] <= q_span[:, None])
            top = jnp.max(jnp.where(visible, scores, jnp.float32(-1e30)), axis=1)
            weights = jnp.where(visible, jnp.exp(scores - top[:, None]), jnp.float32(0.0))
            total = jnp.sum(weights, axis=1)
            out = jnp.dot(weights.astype(jnp.bfloat16), v_head, preferred_element_type=jnp.float32)
            return out / total[:, None]

        return lax.map(one_block, jnp.arange(blocks, dtype=jnp.int32)).reshape(TOKENS, HEAD_DIM)

    outs = lax.map(head_out, jnp.arange(HEADS, dtype=jnp.int32))
    attn = jnp.transpose(outs, (1, 0, 2)).reshape(TOKENS, HEADS * HEAD_DIM).astype(jnp.bfloat16)
    group = HEADS * HEAD_DIM // N_HEAD
    summed = jnp.zeros((TOKENS, D), jnp.float32)
    for index in range(N_HEAD):
        part = jnp.dot(attn[:, index * group:(index + 1) * group], w_out[index * group:(index + 1) * group], preferred_element_type=jnp.float32)
        summed = summed + lax.optimization_barrier(part.astype(jnp.bfloat16)).astype(jnp.float32)
    return summed.astype(jnp.bfloat16)
```

```python
import math

import jax
import jax.numpy as jnp
from jax import lax
from jax.experimental import pallas as pl
from jax.experimental.pallas import tpu as pltpu
from jax.sharding import PartitionSpec as P

HEAD_DIM = 128
SPAN = 64
NX, NZ, NY = 4, 8, 8
ROWS = 256
HELD = 3
BLOCK = NX * ROWS
WCOLS = 192
WROWS = HELD * HEAD_DIM
PIECE = NZ * WCOLS
D = NX * PIECE
MINE = 16
MASKED = -1e30
SCALE = math.log2(math.e) / math.sqrt(HEAD_DIM)
MESH = pl.DeviceIdType.MESH
RIGHT, LEFT = 0, 1
NT = (((1,), (1,)), ((), ()))


def wrap(value, size):
    return lax.rem(value + 2 * size, size)


def kernel(
    q_hbm, k_hbm, v_hbm, w_hbm, slot_ref, doc_ref, out_ref,
    qb, hot, kb, vb, seen, bias, wb, top, acc, ost, ob,
    prod, sib_out, sib_in, rs_out, rs_in,
    own_sem, s1_send, s1_recv, kv_send, kv_recv, wz_send, wz_recv,
    wx_send, wx_recv, wy_send, wy_recv, o_send, o_recv,
    sib_send, sib_recv, rs_send, rs_recv,
):
    ctx, head = lax.axis_index("ctx"), lax.axis_index("head")
    x, z = lax.div(ctx, NZ), lax.rem(ctx, NZ)
    y, core = lax.div(head, 2), lax.rem(head, 2)

    def at_x(to):
        return (to * NZ + z, head)

    def at_z(to):
        return (x * NZ + to, head)

    def at_y(to):
        return (ctx, to * 2 + core)

    sibling = (ctx, y * 2 + 1 - core)
    z_side = (wrap(z + 1, NZ), wrap(z - 1, NZ))
    x_side = (wrap(x + 1, NX), wrap(x - 1, NX))
    y_side = (wrap(y + 1, NY), wrap(y - 1, NY))

    def remote(src, dst, send, recv, device):
        return pltpu.make_async_remote_copy(
            src_ref=src, dst_ref=dst, send_sem=send, recv_sem=recv,
            device_id=device, device_id_type=MESH,
        )

    def head_of(ring):
        return lax.div(ring + 1, 2)

    def columns(ring):
        return pl.ds(pl.multiple_of(head_of(ring) * HEAD_DIM, HEAD_DIM), HEAD_DIM)

    own = [
        pltpu.make_async_copy(w_hbm, wb.at[x, z], own_sem.at[0]),
        pltpu.make_async_copy(k_hbm.at[:, columns(x)], kb.at[z, x], own_sem.at[1]),
        pltpu.make_async_copy(v_hbm.at[:, columns(x)], vb.at[z, x], own_sem.at[2]),
        pltpu.make_async_copy(q_hbm.at[:, columns(x)], qb.at[x], own_sem.at[3]),
    ]
    for copy in own:
        copy.start()

    barrier = pltpu.get_barrier_semaphore()
    peers = [at_x(wrap(x + step, NX)) for step in (1, 2, 3)]
    peers += [at_z(z_side[0]), at_z(z_side[1]), at_y(y_side[0]), at_y(y_side[1]), sibling]
    for peer in peers:
        pl.semaphore_signal(barrier, inc=1, device_id=peer, device_id_type=MESH)
    pl.semaphore_wait(barrier, len(peers))

    def first(kind, step):
        to = wrap(x + step, NX)
        src = (k_hbm, v_hbm, q_hbm)[kind].at[:, columns(to)]
        dst = qb.at[x] if kind == 2 else (kb, vb)[kind].at[z, x]
        return remote(src, dst, s1_send.at[kind, step - 1], s1_recv.at[kind, step - 1], at_x(to))

    def first_arrived(kind, step):
        by = wrap(x - step, NX)
        dst = qb.at[by] if kind == 2 else (kb, vb)[kind].at[z, by]
        remote(dst, dst, s1_send.at[kind, step - 1], s1_recv.at[kind, step - 1], at_x(by)).wait_recv()

    def ring_piece(buf, owner, side, step, whole, cut):
        if step < NZ // 2 - 1:
            return whole(buf, owner)
        return cut(buf, owner, side)

    def w_whole(buf, owner):
        return buf.at[owner]

    def w_cut(buf, owner, side):
        return buf.at[owner, pl.ds(side * (WCOLS // 2), WCOLS // 2)]

    def kv_whole(buf, owner):
        return buf.at[owner]

    def kv_cut(buf, owner, side):
        return buf.at[owner, pl.ds(side * (NX // 2), NX // 2)]

    def toward(side, step):
        return wrap(z - step, NZ) if side == RIGHT else wrap(z + step, NZ)

    def wz(side, step):
        piece = ring_piece(wb.at[x], toward(side, step), side, step, w_whole, w_cut)
        return remote(piece, piece, wz_send.at[side, step], wz_recv.at[side, step], at_z(z_side[side]))

    def wz_arrived(side, step):
        piece = ring_piece(wb.at[x], toward(side, step + 1), side, step, w_whole, w_cut)
        remote(piece, piece, wz_send.at[side, step], wz_recv.at[side, step], at_z(z_side[side])).wait_recv()

    def kv(kind, side, step):
        piece = ring_piece((kb, vb)[kind], toward(side, step), side, step, kv_whole, kv_cut)
        return remote(
            piece, piece, kv_send.at[kind, side, step], kv_recv.at[kind, side, step], at_z(z_side[side])
        )

    def kv_arrived(kind, side, step):
        piece = ring_piece((kb, vb)[kind], toward(side, step + 1), side, step, kv_whole, kv_cut)
        remote(
            piece, piece, kv_send.at[kind, side, step], kv_recv.at[kind, side, step], at_z(z_side[side])
        ).wait_recv()

    order = [z]
    for step in range(1, NZ // 2):
        order += [wrap(z - step, NZ), wrap(z + step, NZ)]
    order += [wrap(z + NZ // 2, NZ)]

    def wx(side, at):
        piece = wb.at[x, order[at]]
        return remote(piece, piece, wx_send.at[side, at], wx_recv.at[side, at], at_x(x_side[side]))

    def wx_arrived(side, at):
        piece = wb.at[x_side[1 - side], order[at]]
        remote(piece, piece, wx_send.at[side, at], wx_recv.at[side, at], at_x(x_side[side])).wait_recv()

    def wy(side, at):
        piece = wb.at[x_side[1 - side], order[at], pl.ds(side * (WCOLS // 2), WCOLS // 2)]
        return remote(piece, piece, wy_send.at[side, at], wy_recv.at[side, at], at_x(x_side[side]))

    def wy_arrived(side, at):
        piece = wb.at[wrap(x + 2, NX), order[at], pl.ds(side * (WCOLS // 2), WCOLS // 2)]
        remote(piece, piece, wy_send.at[side, at], wy_recv.at[side, at], at_x(x_side[side])).wait_recv()

    def spread(at):
        for side in (RIGHT, LEFT):
            wx(side, at).start()

    def hand_on(at):
        for side in (RIGHT, LEFT):
            wx_arrived(side, at)
            wy(side, at).start()

    for kind in (0, 1):
        for step in (1, 2, 3):
            first(kind, step).start()
    own[0].wait()
    for side in (RIGHT, LEFT):
        wz(side, 0).start()
    for step in (1, 2, 3):
        first(2, step).start()
    spread(0)

    rows_at = lax.broadcasted_iota(jnp.int32, (128, 128), 0)
    lanes_at = lax.broadcasted_iota(jnp.int32, (128, 128), 1)
    zero = jnp.zeros((128, 128), jnp.float32)
    slot_row = jnp.broadcast_to(slot_ref[...].astype(jnp.float32), (128, 128))
    doc_row = jnp.broadcast_to(doc_ref[...].astype(jnp.float32), (128, 128))
    clip = jnp.sum(jnp.where(rows_at == lanes_at, slot_row, zero), axis=1, keepdims=True)
    clip = jnp.broadcast_to(clip, (128, 128))
    doc = jnp.sum(jnp.where(clip == lanes_at.astype(jnp.float32), doc_row, zero), axis=1, keepdims=True)
    doc = jnp.broadcast_to(doc, (128, 128))
    start = jnp.sum(jnp.where(doc_row < doc, zero + 1.0, zero), axis=1, keepdims=True)
    start = jnp.broadcast_to(start, (128, 128))
    spans = ROWS // SPAN
    wanted = (lax.div(lanes_at, spans) * NZ + z) * spans + lax.rem(lanes_at, spans)
    chosen = rows_at == wanted
    clip_q = jnp.sum(jnp.where(chosen, clip, zero), axis=0, keepdims=True)
    start_q = jnp.sum(jnp.where(chosen, start, zero), axis=0, keepdims=True)
    visible = (clip <= clip_q) & (clip >= start_q)
    seen[...] = jnp.where(visible, zero, zero + MASKED)

    def expand(zz, unused):
        for at in range(NX * spans):
            slot = (at // spans * NZ + zz) * spans + at % spans
            row = jnp.broadcast_to(seen[pl.ds(slot, 1), :], (SPAN, 128))
            bias[zz, pl.ds(at * SPAN, SPAN), :] = row.astype(jnp.bfloat16)
        return unused

    lax.fori_loop(0, NZ, expand, 0)
    span_at = lax.div(lax.broadcasted_iota(jnp.int32, (ROWS, 128), 0), SPAN)
    lane_at = lax.broadcasted_iota(jnp.int32, (ROWS, 128), 1)
    for part in range(NX):
        hot[part] = jnp.where(lane_at == span_at + part * spans, 1.0, 0.0).astype(jnp.bfloat16)
    top[...] = jnp.full(top.shape, MASKED, jnp.float32)
    acc[...] = jnp.zeros(acc.shape, jnp.float32)

    def tile(block, part):
        q_all = jnp.concatenate([qb[part], hot[part]], axis=1)
        k_all = jnp.concatenate([kb[block].reshape(BLOCK, HEAD_DIM), bias[block]], axis=1)
        v_all = vb[block].reshape(BLOCK, HEAD_DIM)
        v_all = jnp.concatenate([v_all, jnp.ones((BLOCK, 128), jnp.bfloat16)], axis=1)
        scores = lax.dot_general(q_all, k_all, NT, preferred_element_type=jnp.float32)
        old = top[part]
        new = jnp.maximum(old, jnp.broadcast_to(jnp.max(scores, axis=1, keepdims=True), old.shape))
        scaled = new * SCALE
        weights = jnp.exp2(scores * SCALE - jnp.concatenate([scaled] * (BLOCK // 128), axis=1))
        shrink = jnp.exp2(old * SCALE - scaled)
        fresh = jnp.dot(weights.astype(jnp.bfloat16), v_all, preferred_element_type=jnp.float32)
        acc[part] = acc[part] * jnp.concatenate([shrink, shrink], axis=1) + fresh
        top[part] = new

    def attend_two(one, other):
        def body(at, unused):
            tile(jnp.where(at < NX, one, other), lax.rem(at, NX))
            return unused
        lax.fori_loop(0, 2 * NX, body, 0)

    def w_step(step):
        for side in (RIGHT, LEFT):
            wz_arrived(side, step)
            wz(side, step + 1).start()
        spread(2 * step + 1)
        spread(2 * step + 2)

    w_step(0)
    for kind in (0, 1):
        for step in (1, 2, 3):
            first_arrived(kind, step)
        own[1 + kind].wait()
        for side in (RIGHT, LEFT):
            kv(kind, side, 0).start()
    w_step(1)
    for step in (1, 2, 3):
        first_arrived(2, step)
    own[3].wait()

    def attend_own(part, unused):
        tile(z, part)
        return unused

    lax.fori_loop(0, NX, attend_own, 0)
    w_step(2)
    for side in (RIGHT, LEFT):
        wz_arrived(side, 3)
    spread(7)

    for step in (0, 1, 2):
        for kind in (0, 1):
            for side in (RIGHT, LEFT):
                kv_arrived(kind, side, step)
                kv(kind, side, step + 1).start()
        attend_two(wrap(z - step - 1, NZ), wrap(z + step + 1, NZ))
        if step < 2:
            for at in range(4 * step, 4 * step + 4):
                hand_on(at)
    for kind in (0, 1):
        for side in (RIGHT, LEFT):
            kv_arrived(kind, side, 3)

    mine = head_of(x)

    def gives(part):
        half = (x == 1) & (part < 2) | (x == 2) & (part >= 2)
        return (x == 0) | (x == 3) | half

    def answer(part):
        return remote(ost.at[part], ob.at[mine], o_send.at[part], o_recv.at[mine], at_x(part))

    def attend_last(part, unused):
        tile(wrap(z + NZ // 2, NZ), part)
        result = acc[part]
        result = (result[:, :HEAD_DIM] / result[:, HEAD_DIM:]).astype(jnp.bfloat16)
        ost[part] = result

        @pl.when(gives(part) & (part != x))
        def _():
            answer(part).start()

        @pl.when(gives(part) & (part == x))
        def _():
            ob[mine] = result

        return unused

    lax.fori_loop(0, NX, attend_last, 0)
    for side in (RIGHT, LEFT):
        for at in range(NZ):
            wy_arrived(side, at)
    for index in range(HELD):
        giver = jnp.where(x < 2, 1, 2) if index == 1 else (0, 0, 3)[index]

        @pl.when(giver != x)
        def _():
            remote(
                ost.at[0], ob.at[index], o_send.at[0], o_recv.at[index], at_x(wrap(x + 1, NX))
            ).wait_recv()

    attn = jnp.concatenate([ob[0], ob[1], ob[2]], axis=1)

    def to_sibling(piece):
        return remote(sib_out.at[piece], sib_in.at[piece], sib_send.at[piece], sib_recv.at[piece], sibling)

    for piece in range(NX):
        part = lax.dot_general(
            attn, wb[piece].reshape(PIECE, WROWS), NT, preferred_element_type=jnp.float32
        )
        prod[piece] = part.reshape(NY, 2, MINE, PIECE)
        sib_out[piece] = prod[piece, :, 1 - core].astype(jnp.bfloat16)
        to_sibling(piece).start()

    def rs(side, step, piece):
        return remote(
            rs_out.at[side, step, piece], rs_in.at[side, step, piece],
            rs_send.at[side, step, piece], rs_recv.at[side, step, piece], at_y(y_side[side]),
        )

    def here(piece, owner):
        return prod[piece, owner, core] + sib_in[piece, owner].astype(jnp.float32)

    def travels(side, step, piece):
        return step > 0 or piece // (NX // 2) == side

    for step in range(NY // 2):
        for piece in range(NX):
            if step == 0:
                to_sibling(piece).wait_recv()
            for side in (RIGHT, LEFT):
                if not travels(side, step, piece):
                    continue
                away = NY // 2 - step
                total = here(piece, wrap(y + away if side == RIGHT else y - away, NY))
                if step > 0 and travels(side, step - 1, piece):
                    rs(side, step - 1, piece).wait_recv()
                    total = total + rs_in[side, step - 1, piece].astype(jnp.float32)
                rs_out[side, step, piece] = total.astype(jnp.bfloat16)
                rs(side, step, piece).start()
    for piece in range(NX):
        total = here(piece, y)
        for side in (RIGHT, LEFT):
            rs(side, NY // 2 - 1, piece).wait_recv()
            total = total + rs_in[side, NY // 2 - 1, piece].astype(jnp.float32)
        out_ref[:, pl.ds(piece * PIECE, PIECE)] = total.astype(jnp.bfloat16)

    for kind in (0, 1, 2):
        for step in (1, 2, 3):
            first(kind, step).wait_send()
    for side in (RIGHT, LEFT):
        for step in range(NZ // 2):
            wz(side, step).wait_send()
            for kind in (0, 1):
                kv(kind, side, step).wait_send()
        for at in range(NZ):
            wx(side, at).wait_send()
            wy(side, at).wait_send()
    for part in range(NX):
        @pl.when(gives(part) & (part != x))
        def _():
            answer(part).wait_send()
    for piece in range(NX):
        to_sibling(piece).wait_send()
    for step in range(NY // 2):
        for piece in range(NX):
            for side in (RIGHT, LEFT):
                if travels(side, step, piece):
                    rs(side, step, piece).wait_send()


def local(query, keys, values, span_slot, span_doc, w_out):
    whole = pl.BlockSpec(memory_space=pltpu.VMEM)
    remote = pl.BlockSpec(memory_space=pl.ANY)
    bf16, f32 = jnp.bfloat16, jnp.float32
    dma = pltpu.SemaphoreType.DMA
    return pl.pallas_call(
        kernel,
        out_shape=jax.ShapeDtypeStruct((MINE, D), bf16),
        in_specs=[remote] * 4 + [whole] * 2,
        out_specs=whole,
        scratch_shapes=[
            pltpu.VMEM((NX, ROWS, HEAD_DIM), bf16),
            pltpu.VMEM((NX, ROWS, 128), bf16),
            pltpu.VMEM((NZ, NX, ROWS, HEAD_DIM), bf16),
            pltpu.VMEM((NZ, NX, ROWS, HEAD_DIM), bf16),
            pltpu.VMEM((128, 128), f32),
            pltpu.VMEM((NZ, BLOCK, 128), bf16),
            pltpu.VMEM((NX, NZ, WCOLS, WROWS), bf16),
            pltpu.VMEM((NX, ROWS, 128), f32),
            pltpu.VMEM((NX, ROWS, 256), f32),
            pltpu.VMEM((NX, ROWS, HEAD_DIM), bf16),
            pltpu.VMEM((HELD, ROWS, HEAD_DIM), bf16),
            pltpu.VMEM((NX, NY, 2, MINE, PIECE), f32),
            pltpu.VMEM((NX, NY, MINE, PIECE), bf16),
            pltpu.VMEM((NX, NY, MINE, PIECE), bf16),
            pltpu.VMEM((2, NY // 2, NX, MINE, PIECE), bf16),
            pltpu.VMEM((2, NY // 2, NX, MINE, PIECE), bf16),
            dma((4,)),
            dma((3, 3)), dma((3, 3)),
            dma((2, 2, NZ // 2)), dma((2, 2, NZ // 2)),
            dma((2, NZ // 2)), dma((2, NZ // 2)),
            dma((2, NZ)), dma((2, NZ)),
            dma((2, NZ)), dma((2, NZ)),
            dma((NX,)), dma((HELD,)),
            dma((NX,)), dma((NX,)),
            dma((2, NY // 2, NX)), dma((2, NY // 2, NX)),
        ],
        compiler_params=pltpu.CompilerParams(
            collective_id=0, has_side_effects=True, vmem_limit_bytes=56 << 20
        ),
        cost_estimate=pl.CostEstimate(
            flops=2 * BLOCK * 8192 * 512 + 2 * ROWS * WROWS * D,
            bytes_accessed=1 << 21, transcendentals=BLOCK * 8192,
        ),
    )(query, keys, values, w_out.T, span_slot.reshape(1, 128), span_doc.reshape(1, 128))


def solution(mesh):
    placed = (P("ctx", "head"), P("ctx", "head"), P("ctx", "head"), P(), P(), P("head", "ctx"))
    return jax.shard_map(
        local, mesh=mesh, in_specs=placed, out_specs=P(("ctx", "head"), None), check_vma=False
    )
```

```python
import math

import jax
import jax.numpy as jnp
from jax import lax
from jax.experimental import pallas as pl
from jax.experimental.pallas import tpu as pltpu
from jax.sharding import PartitionSpec as P

HEAD_DIM = 128
SPAN = 64
NX, NZ, NY = 4, 8, 8
ROWS = 256
HELD = 3
BLOCK = NX * ROWS
WCOLS = 192
WROWS = HELD * HEAD_DIM
PIECE = NZ * WCOLS
D = NX * PIECE
MINE = 16
MASKED = -1e30
LOWEST = -2e30
CUT = 96
SCALE = math.log2(math.e) / math.sqrt(HEAD_DIM)
MESH = pl.DeviceIdType.MESH
RIGHT, LEFT = 0, 1
NT = (((1,), (1,)), ((), ()))


def wrap(value, size):
    return lax.rem(value + 2 * size, size)


def kernel(
    q_hbm, k_hbm, v_hbm, w_hbm, slot_ref, doc_ref, out_ref,
    qb, hot, kb, vb, seen, bias, wb, top, acc, ost, ob, stat_out, stat_in,
    prod, sib_out, sib_in, rs_out, rs_in,
    own_sem, s1_send, s1_recv, kv0_send, kv0_recv, kv_send, kv_recv, wz_send, wz_recv,
    wx_send, wx_recv, wy_send, wy_recv, o_send, o_recv, stat_send, stat_recv,
    sib_send, sib_recv, rs_send, rs_recv,
):
    ctx, head = lax.axis_index("ctx"), lax.axis_index("head")
    x, z = lax.div(ctx, NZ), lax.rem(ctx, NZ)
    y, core = lax.div(head, 2), lax.rem(head, 2)

    def at_x(to):
        return (to * NZ + z, head)

    def at_z(to):
        return (x * NZ + to, head)

    def at_y(to):
        return (ctx, to * 2 + core)

    sibling = (ctx, y * 2 + 1 - core)
    z_side = (wrap(z + 1, NZ), wrap(z - 1, NZ))
    x_side = (wrap(x + 1, NX), wrap(x - 1, NX))
    y_side = (wrap(y + 1, NY), wrap(y - 1, NY))

    def remote(src, dst, send, recv, device):
        return pltpu.make_async_remote_copy(
            src_ref=src, dst_ref=dst, send_sem=send, recv_sem=recv,
            device_id=device, device_id_type=MESH,
        )

    def is_full(ring):
        edge = jnp.where((ring == 0) | (ring == NX - 1), 1, 0)
        return edge + core == 1

    def head_of(ring):
        return jnp.where(is_full(ring), 2 * lax.div(ring, 2), 1)

    def columns(ring):
        return pl.ds(pl.multiple_of(head_of(ring) * HEAD_DIM, HEAD_DIM), HEAD_DIM)

    def place(ring, source):
        return jnp.where(is_full(ring), source, lax.rem(source, 2))

    def wants(ring, source):
        return is_full(ring) | (lax.div(ring, 2) == lax.div(source, 2))

    full = is_full(x)
    not_full = jnp.logical_not(full)
    halves = jnp.where(full, 2, 1)

    own = [
        pltpu.make_async_copy(w_hbm, wb.at[x, z], own_sem.at[0]),
        pltpu.make_async_copy(k_hbm.at[:, columns(x)], kb.at[z, place(x, x)], own_sem.at[1]),
        pltpu.make_async_copy(v_hbm.at[:, columns(x)], vb.at[z, place(x, x)], own_sem.at[2]),
        pltpu.make_async_copy(q_hbm.at[:, columns(x)], qb.at[x], own_sem.at[3]),
    ]
    for copy in own:
        copy.start()

    barrier = pltpu.get_barrier_semaphore()
    peers = [at_x(wrap(x + step, NX)) for step in (1, 2, 3)]
    peers += [at_z(z_side[0]), at_z(z_side[1]), at_y(y_side[0]), at_y(y_side[1]), sibling]
    for peer in peers:
        pl.semaphore_signal(barrier, inc=1, device_id=peer, device_id_type=MESH)
    pl.semaphore_wait(barrier, len(peers))

    def first(kind, step):
        to = wrap(x + step, NX)
        src = (k_hbm, v_hbm, q_hbm)[kind].at[:, columns(to)]
        dst = qb.at[x] if kind == 2 else (kb, vb)[kind].at[z, place(to, x)]
        return remote(src, dst, s1_send.at[kind, step - 1], s1_recv.at[kind, step - 1], at_x(to))

    def first_arrived(kind, step):
        by = wrap(x - step, NX)
        dst = qb.at[by] if kind == 2 else (kb, vb)[kind].at[z, place(x, by)]
        remote(dst, dst, s1_send.at[kind, step - 1], s1_recv.at[kind, step - 1], at_x(by)).wait_recv()

    def toward(side, step):
        return wrap(z - step, NZ) if side == RIGHT else wrap(z + step, NZ)

    def wz_piece(side, owner, step):
        if step < NZ // 2 - 1:
            return wb.at[x, owner]
        return wb.at[x, owner, pl.ds(side * (WCOLS // 2), WCOLS // 2)]

    def wz(side, step):
        piece = wz_piece(side, toward(side, step), step)
        return remote(piece, piece, wz_send.at[side, step], wz_recv.at[side, step], at_z(z_side[side]))

    def wz_arrived(side, step):
        piece = wz_piece(side, toward(side, step + 1), step)
        remote(piece, piece, wz_send.at[side, step], wz_recv.at[side, step], at_z(z_side[side])).wait_recv()

    def kv0(kind, side, at, owner):
        piece = (kb, vb)[kind].at[owner, at]
        return remote(
            piece, piece, kv0_send.at[kind, side, at], kv0_recv.at[kind, side, at], at_z(z_side[side])
        )

    def kv(kind, side, step, half, owner):
        piece = (kb, vb)[kind].at[owner, pl.ds(2 * half, 2)]
        return remote(
            piece, piece, kv_send.at[kind, side, step - 1, half], kv_recv.at[kind, side, step - 1, half],
            at_z(z_side[side]),
        )

    def kv3(kind, side, owner, count):
        piece = (kb, vb)[kind].at[owner, pl.ds(side * count, count)]
        return remote(
            piece, piece, kv_send.at[kind, side, 2, 0], kv_recv.at[kind, side, 2, 0], at_z(z_side[side])
        )

    order = [z]
    for step in range(1, NZ // 2):
        order += [wrap(z - step, NZ), wrap(z + step, NZ)]
    order += [wrap(z + NZ // 2, NZ)]

    def wx(side, at):
        piece = wb.at[x, order[at]]
        return remote(piece, piece, wx_send.at[side, at], wx_recv.at[side, at], at_x(x_side[side]))

    def wx_arrived(side, at):
        piece = wb.at[x_side[1 - side], order[at]]
        remote(piece, piece, wx_send.at[side, at], wx_recv.at[side, at], at_x(x_side[side])).wait_recv()

    def wy_rows(side):
        return pl.ds(0, CUT) if side == RIGHT else pl.ds(CUT, WCOLS - CUT)

    def wy(side, at):
        piece = wb.at[x_side[1 - side], order[at], wy_rows(side)]
        return remote(piece, piece, wy_send.at[side, at], wy_recv.at[side, at], at_x(x_side[side]))

    def wy_arrived(side, at):
        piece = wb.at[wrap(x + 2, NX), order[at], wy_rows(side)]
        remote(piece, piece, wy_send.at[side, at], wy_recv.at[side, at], at_x(x_side[side])).wait_recv()

    def spread(at):
        for side in (RIGHT, LEFT):
            wx(side, at).start()

    def hand_on(at):
        for side in (RIGHT, LEFT):
            wx_arrived(side, at)
            wy(side, at).start()

    for kind in (0, 1):
        for step in (1, 3, 2):
            @pl.when(wants(wrap(x + step, NX), x))
            def _():
                first(kind, step).start()
    own[0].wait()
    for side in (RIGHT, LEFT):
        wz(side, 0).start()
    for kind in (0, 1):
        own[1 + kind].wait()
        for side in (RIGHT, LEFT):
            kv0(kind, side, place(x, x), z).start()
    for step in (1, 3, 2):
        first(2, step).start()
    spread(0)

    rows_at = lax.broadcasted_iota(jnp.int32, (128, 128), 0)
    lanes_at = lax.broadcasted_iota(jnp.int32, (128, 128), 1)
    zero = jnp.zeros((128, 128), jnp.float32)
    slot_row = jnp.broadcast_to(slot_ref[...].astype(jnp.float32), (128, 128))
    doc_row = jnp.broadcast_to(doc_ref[...].astype(jnp.float32), (128, 128))
    clip = jnp.sum(jnp.where(rows_at == lanes_at, slot_row, zero), axis=1, keepdims=True)
    clip = jnp.broadcast_to(clip, (128, 128))
    doc = jnp.sum(jnp.where(clip == lanes_at.astype(jnp.float32), doc_row, zero), axis=1, keepdims=True)
    doc = jnp.broadcast_to(doc, (128, 128))
    start = jnp.sum(jnp.where(doc_row < doc, zero + 1.0, zero), axis=1, keepdims=True)
    start = jnp.broadcast_to(start, (128, 128))
    spans = ROWS // SPAN
    wanted = (lax.div(lanes_at, spans) * NZ + z) * spans + lax.rem(lanes_at, spans)
    chosen = rows_at == wanted
    clip_q = jnp.sum(jnp.where(chosen, clip, zero), axis=0, keepdims=True)
    start_q = jnp.sum(jnp.where(chosen, start, zero), axis=0, keepdims=True)
    visible = (clip <= clip_q) & (clip >= start_q)
    seen[...] = jnp.where(visible, zero, zero + MASKED)

    def expand(zz, unused):
        for at in range(NX):
            source = jnp.where(full, at, lax.rem(2 * lax.div(x, 2) + at, NX))
            for span in range(spans):
                row = seen[pl.ds((source * NZ + zz) * spans + span, 1), :]
                row = jnp.broadcast_to(row, (SPAN, 128)).astype(jnp.bfloat16)
                bias[zz, at, pl.ds(span * SPAN, SPAN), :] = row
        return unused

    lax.fori_loop(0, NZ, expand, 0)
    span_at = lax.div(lax.broadcasted_iota(jnp.int32, (ROWS, 128), 0), SPAN)
    lane_at = lax.broadcasted_iota(jnp.int32, (ROWS, 128), 1)
    for part in range(NX):
        hot[part] = jnp.where(lane_at == span_at + part * spans, 1.0, 0.0).astype(jnp.bfloat16)
    top[...] = jnp.full(top.shape, LOWEST, jnp.float32)
    acc[...] = jnp.zeros(acc.shape, jnp.float32)

    def attend(block, half, tiles, parts):
        count = tiles * ROWS
        held = pl.ds(2 * half, tiles)
        k_all = jnp.concatenate(
            [kb[block, held].reshape(count, HEAD_DIM), bias[block, held].reshape(count, 128)], axis=1
        )
        v_all = jnp.concatenate(
            [vb[block, held].reshape(count, HEAD_DIM), jnp.ones((count, 128), jnp.bfloat16)], axis=1
        )
        for part in parts:
            q_all = jnp.concatenate([qb[part], hot[part]], axis=1)
            scores = lax.dot_general(q_all, k_all, NT, preferred_element_type=jnp.float32)
            old = top[part]
            new = jnp.maximum(old, jnp.broadcast_to(jnp.max(scores, axis=1, keepdims=True), old.shape))
            scaled = new * SCALE
            weights = jnp.exp2(scores * SCALE - jnp.concatenate([scaled] * (count // 128), axis=1))
            shrink = jnp.exp2(old * SCALE - scaled)
            fresh = jnp.dot(weights.astype(jnp.bfloat16), v_all, preferred_element_type=jnp.float32)
            acc[part] = acc[part] * jnp.concatenate([shrink, shrink], axis=1) + fresh
            top[part] = new

    def w_step(step):
        for side in (RIGHT, LEFT):
            wz_arrived(side, step)
            wz(side, step + 1).start()
        spread(2 * step + 1)
        spread(2 * step + 2)

    w_step(0)
    for step in (1, 3, 2):
        by = wrap(x - step, NX)

        @pl.when(wants(x, by))
        def _():
            for kind in (0, 1):
                first_arrived(kind, step)
                for side in (RIGHT, LEFT):
                    kv0(kind, side, place(x, by), z).start()
    w_step(1)
    for step in (1, 2, 3):
        first_arrived(2, step)
    own[3].wait()

    def attend_own(half, unused):
        attend(z, half, 2, range(NX))
        return unused

    lax.fori_loop(0, halves, attend_own, 0)
    w_step(2)
    for side in (RIGHT, LEFT):
        wz_arrived(side, 3)
    spread(7)

    for step in (0, 1, 2):
        def half_step(half, unused):
            for kind in (0, 1):
                for side in (RIGHT, LEFT):
                    owner = toward(side, step + 1)
                    if step == 0:
                        for at in (0, 1):
                            kv0(kind, side, 2 * half + at, owner).wait_recv()
                    else:
                        kv(kind, side, step, half, owner).wait_recv()
                    if step < 2:
                        kv(kind, side, step + 1, half, owner).start()
                    else:
                        @pl.when(full & (half == side))
                        def _():
                            kv3(kind, side, owner, 2).start()

                        @pl.when(not_full)
                        def _():
                            kv3(kind, side, owner, 1).start()

            def body(at, unused):
                attend(jnp.where(at == 0, toward(RIGHT, step + 1), toward(LEFT, step + 1)), half, 2, range(NX))
                return unused

            lax.fori_loop(0, 2, body, 0)
            return unused

        lax.fori_loop(0, halves, half_step, 0)
        if step < 2:
            for at in range(4 * step, 4 * step + 4):
                hand_on(at)

    def answer(part):
        return remote(ost.at[part], ob.at[x], o_send.at[part], o_recv.at[x], at_x(part))

    def answer_stat(part):
        return remote(
            stat_out.at[part], stat_in.at[x], stat_send.at[part], stat_recv.at[x], at_x(part)
        )

    eye = rows_at == lanes_at

    def finish(part):
        total = acc[part]
        result = (total[:, :HEAD_DIM] / total[:, HEAD_DIM:]).astype(jnp.bfloat16)
        ost[part] = result

        @pl.when(part != x)
        def _():
            answer(part).start()

        @pl.when(part == x)
        def _():
            ob[x] = result

        @pl.when(not_full)
        def _():
            scaled = top[part] * SCALE
            sums = total[:, HEAD_DIM:]
            rows = []
            for which in (scaled, sums):
                for at in (0, 128):
                    rows.append(jnp.sum(jnp.where(eye, which[at:at + 128], zero), axis=0, keepdims=True))
            stats = jnp.concatenate(rows + [zero[:4]], axis=0)
            stat_out[part] = stats

            @pl.when(part != x)
            def _():
                answer_stat(part).start()

            @pl.when(part == x)
            def _():
                stat_in[x] = stats

    last = wrap(z + NZ // 2, NZ)

    def arrive_last(count):
        for kind in (0, 1):
            for side in (RIGHT, LEFT):
                kv3(kind, side, last, count).wait_recv()

    def end_with(tiles):
        def body(pair, unused):
            parts = (2 * pair, 2 * pair + 1)
            attend(last, 0, tiles, parts)
            for part in parts:
                finish(part)
            return unused
        lax.fori_loop(0, 2, body, 0)

    @pl.when(full)
    def _():
        arrive_last(2)
        end_with(4)

    @pl.when(not_full)
    def _():
        arrive_last(1)
        end_with(2)

    for giver in range(NX):
        @pl.when(giver != x)
        def _():
            remote(ost.at[0], ob.at[giver], o_send.at[0], o_recv.at[giver], at_x(x_side[0])).wait_recv()

            @pl.when(jnp.logical_not(is_full(giver)))
            def _():
                remote(
                    stat_out.at[0], stat_in.at[giver], stat_send.at[0], stat_recv.at[giver], at_x(x_side[0])
                ).wait_recv()

    def column(stats, first_row):
        parts = []
        for at in (first_row, first_row + 1):
            row = jnp.broadcast_to(stats[at:at + 1], (128, 128))
            whole = jnp.sum(jnp.where(eye, row, zero), axis=1, keepdims=True)
            parts.append(jnp.broadcast_to(whole, (128, 128)))
        return jnp.concatenate(parts, axis=0)

    one, two = 1 - core, 2 + core
    top_one, top_two = column(stat_in[one], 0), column(stat_in[two], 0)
    best = jnp.maximum(top_one, top_two)
    share_one = column(stat_in[one], 2) * jnp.exp2(top_one - best)
    share_two = column(stat_in[two], 2) * jnp.exp2(top_two - best)
    middle = ob[one].astype(jnp.float32) * share_one + ob[two].astype(jnp.float32) * share_two
    middle = (middle / (share_one + share_two)).astype(jnp.bfloat16)
    attn = jnp.concatenate([ob[core], middle, ob[NX - 1 - core]], axis=1)

    def to_sibling(piece):
        return remote(sib_out.at[piece], sib_in.at[piece], sib_send.at[piece], sib_recv.at[piece], sibling)

    def rs(side, step, piece):
        return remote(
            rs_out.at[side, step, piece], rs_in.at[side, step, piece],
            rs_send.at[side, step, piece], rs_recv.at[side, step, piece], at_y(y_side[side]),
        )

    def here(piece, owner):
        return prod[piece, owner, core] + sib_in[piece, owner].astype(jnp.float32)

    def travels(side, step, piece):
        return step > 0 or piece // (NX // 2) == side

    def pass_on(side, step, piece):
        away = NY // 2 - step
        total = here(piece, wrap(y + away if side == RIGHT else y - away, NY))
        if step > 0 and travels(side, step - 1, piece):
            rs(side, step - 1, piece).wait_recv()
            total = total + rs_in[side, step - 1, piece].astype(jnp.float32)
        rs_out[side, step, piece] = total.astype(jnp.bfloat16)
        rs(side, step, piece).start()

    def begin(piece):
        to_sibling(piece).wait_recv()
        side = piece // (NX // 2)
        pass_on(side, 0, piece)
        pass_on(1 - side, 1, piece)

    for side in (RIGHT, LEFT):
        for at in range(NZ):
            wy_arrived(side, at)
    turn = (0, 2, 1, 3)
    for index, piece in enumerate(turn):
        part = lax.dot_general(
            attn, wb[piece].reshape(PIECE, WROWS), NT, preferred_element_type=jnp.float32
        )
        prod[piece] = part.reshape(NY, 2, MINE, PIECE)
        sib_out[piece] = prod[piece, :, 1 - core].astype(jnp.bfloat16)
        to_sibling(piece).start()
        if index:
            begin(turn[index - 1])
    begin(turn[-1])
    late = ((2, 3, 0, 1), (0, 1, 2, 3))
    for at in (0, 1):
        for side in (RIGHT, LEFT):
            pass_on(side, 1, late[side][2 + at])
    for step in range(2, NY // 2):
        for at in range(NX):
            for side in (RIGHT, LEFT):
                pass_on(side, step, late[side][at])
    for piece in (2, 0, 3, 1):
        total = here(piece, y)
        for side in (RIGHT, LEFT):
            rs(side, NY // 2 - 1, piece).wait_recv()
            total = total + rs_in[side, NY // 2 - 1, piece].astype(jnp.float32)
        out_ref[:, pl.ds(piece * PIECE, PIECE)] = total.astype(jnp.bfloat16)

    for step in (1, 2, 3):
        first(2, step).wait_send()

        @pl.when(wants(wrap(x + step, NX), x))
        def _():
            for kind in (0, 1):
                first(kind, step).wait_send()

    def sent(half, unused):
        for kind in (0, 1):
            for side in (RIGHT, LEFT):
                for at in (0, 1):
                    kv0(kind, side, 2 * half + at, z).wait_send()
                for step in (1, 2):
                    kv(kind, side, step, half, z).wait_send()
        return unused

    lax.fori_loop(0, halves, sent, 0)
    for kind in (0, 1):
        for side in (RIGHT, LEFT):
            @pl.when(full)
            def _():
                kv3(kind, side, z, 2).wait_send()

            @pl.when(not_full)
            def _():
                kv3(kind, side, z, 1).wait_send()
    for side in (RIGHT, LEFT):
        for step in range(NZ // 2):
            wz(side, step).wait_send()
        for at in range(NZ):
            wx(side, at).wait_send()
            wy(side, at).wait_send()
    for part in range(NX):
        @pl.when(part != x)
        def _():
            answer(part).wait_send()

            @pl.when(not_full)
            def _():
                answer_stat(part).wait_send()
    for piece in range(NX):
        to_sibling(piece).wait_send()
    for step in range(NY // 2):
        for piece in range(NX):
            for side in (RIGHT, LEFT):
                if travels(side, step, piece):
                    rs(side, step, piece).wait_send()


def local(query, keys, values, span_slot, span_doc, w_out):
    whole = pl.BlockSpec(memory_space=pltpu.VMEM)
    remote = pl.BlockSpec(memory_space=pl.ANY)
    bf16, f32 = jnp.bfloat16, jnp.float32
    dma = pltpu.SemaphoreType.DMA
    return pl.pallas_call(
        kernel,
        out_shape=jax.ShapeDtypeStruct((MINE, D), bf16),
        in_specs=[remote] * 4 + [whole] * 2,
        out_specs=whole,
        scratch_shapes=[
            pltpu.VMEM((NX, ROWS, HEAD_DIM), bf16),
            pltpu.VMEM((NX, ROWS, 128), bf16),
            pltpu.VMEM((NZ, NX, ROWS, HEAD_DIM), bf16),
            pltpu.VMEM((NZ, NX, ROWS, HEAD_DIM), bf16),
            pltpu.VMEM((128, 128), f32),
            pltpu.VMEM((NZ, NX, ROWS, 128), bf16),
            pltpu.VMEM((NX, NZ, WCOLS, WROWS), bf16),
            pltpu.VMEM((NX, ROWS, 128), f32),
            pltpu.VMEM((NX, ROWS, 256), f32),
            pltpu.VMEM((NX, ROWS, HEAD_DIM), bf16),
            pltpu.VMEM((NX, ROWS, HEAD_DIM), bf16),
            pltpu.VMEM((NX, 8, 128), f32),
            pltpu.VMEM((NX, 8, 128), f32),
            pltpu.VMEM((NX, NY, 2, MINE, PIECE), f32),
            pltpu.VMEM((NX, NY, MINE, PIECE), bf16),
            pltpu.VMEM((NX, NY, MINE, PIECE), bf16),
            pltpu.VMEM((2, NY // 2, NX, MINE, PIECE), bf16),
            pltpu.VMEM((2, NY // 2, NX, MINE, PIECE), bf16),
            dma((4,)),
            dma((3, 3)), dma((3, 3)),
            dma((2, 2, NX)), dma((2, 2, NX)),
            dma((2, 2, 3, 2)), dma((2, 2, 3, 2)),
            dma((2, NZ // 2)), dma((2, NZ // 2)),
            dma((2, NZ)), dma((2, NZ)),
            dma((2, NZ)), dma((2, NZ)),
            dma((NX,)), dma((NX,)),
            dma((NX,)), dma((NX,)),
            dma((NX,)), dma((NX,)),
            dma((2, NY // 2, NX)), dma((2, NY // 2, NX)),
        ],
        compiler_params=pltpu.CompilerParams(
            collective_id=0, has_side_effects=True, vmem_limit_bytes=56 << 20
        ),
        cost_estimate=pl.CostEstimate(
            flops=2 * BLOCK * 8192 * 512 + 2 * ROWS * WROWS * D,
            bytes_accessed=1 << 21, transcendentals=BLOCK * 8192,
        ),
    )(query, keys, values, w_out.T, span_slot.reshape(1, 128), span_doc.reshape(1, 128))


def solution(mesh):
    placed = (P("ctx", "head"), P("ctx", "head"), P("ctx", "head"), P(), P(), P("head", "ctx"))
    return jax.shard_map(
        local, mesh=mesh, in_specs=placed, out_specs=P(("ctx", "head"), None), check_vma=False
    )
```

```python
import math

import jax
import jax.numpy as jnp
from jax import lax
from jax.experimental import pallas as pl
from jax.experimental.pallas import tpu as pltpu
from jax.sharding import PartitionSpec as P

HEAD_DIM = 128
SPAN = 64
NX, NZ, NY = 4, 8, 8
ROWS = 256
HELD = 3
BLOCK = NX * ROWS
WCOLS = 192
WROWS = HELD * HEAD_DIM
PIECE = NZ * WCOLS
D = NX * PIECE
MINE = 16
MASKED = -1e30
LOWEST = -2e30
CUT = 96
SCALE = math.log2(math.e) / math.sqrt(HEAD_DIM)
MESH = pl.DeviceIdType.MESH
RIGHT, LEFT = 0, 1
NT = (((1,), (1,)), ((), ()))


def wrap(value, size):
    return lax.rem(value + 2 * size, size)


def kernel(
    q_hbm, k_hbm, v_hbm, w_hbm, slot_ref, doc_ref, out_ref,
    qb, hot, kb, vb, seen, bias, wb, top, acc, ost, ob, stat_out, stat_in,
    prod, sib_out, sib_in, rs_out, rs_in,
    own_sem, s1_send, s1_recv, kv_send, kv_recv, wz_send, wz_recv,
    wx_send, wx_recv, wy_send, wy_recv, o_send, o_recv, stat_send, stat_recv,
    sib_send, sib_recv, rs_send, rs_recv,
):
    ctx, head = lax.axis_index("ctx"), lax.axis_index("head")
    x, z = lax.div(ctx, NZ), lax.rem(ctx, NZ)
    y, core = lax.div(head, 2), lax.rem(head, 2)

    def at_x(to):
        return (to * NZ + z, head)

    def at_z(to):
        return (x * NZ + to, head)

    def at_y(to):
        return (ctx, to * 2 + core)

    sibling = (ctx, y * 2 + 1 - core)
    z_side = (wrap(z + 1, NZ), wrap(z - 1, NZ))
    x_side = (wrap(x + 1, NX), wrap(x - 1, NX))
    y_side = (wrap(y + 1, NY), wrap(y - 1, NY))

    def remote(src, dst, send, recv, device):
        return pltpu.make_async_remote_copy(
            src_ref=src, dst_ref=dst, send_sem=send, recv_sem=recv,
            device_id=device, device_id_type=MESH,
        )

    def is_full(ring):
        edge = jnp.where((ring == 0) | (ring == NX - 1), 1, 0)
        return edge + core == 1

    def head_of(ring):
        return jnp.where(is_full(ring), 2 * lax.div(ring, 2), 1)

    def columns(ring):
        return pl.ds(pl.multiple_of(head_of(ring) * HEAD_DIM, HEAD_DIM), HEAD_DIM)

    def place(ring, step):
        return jnp.where(is_full(ring), (1, 3, 2)[step - 1], 1)

    def wants(ring, source):
        return is_full(ring) | (lax.div(ring, 2) == lax.div(source, 2))

    full = is_full(x)
    not_full = jnp.logical_not(full)
    halves = jnp.where(full, 2, 1)
    lead = jnp.where(full, 1, 0)

    own = [
        pltpu.make_async_copy(w_hbm, wb.at[x, z], own_sem.at[0]),
        pltpu.make_async_copy(k_hbm.at[:, columns(x)], kb.at[z, 0], own_sem.at[1]),
        pltpu.make_async_copy(v_hbm.at[:, columns(x)], vb.at[z, 0], own_sem.at[2]),
        pltpu.make_async_copy(q_hbm.at[:, columns(x)], qb.at[x], own_sem.at[3]),
    ]
    for copy in own:
        copy.start()

    barrier = pltpu.get_barrier_semaphore()
    peers = [at_x(wrap(x + step, NX)) for step in (1, 2, 3)]
    peers += [at_z(z_side[0]), at_z(z_side[1]), at_y(y_side[0]), at_y(y_side[1]), sibling]
    for peer in peers:
        pl.semaphore_signal(barrier, inc=1, device_id=peer, device_id_type=MESH)
    pl.semaphore_wait(barrier, len(peers))

    def first(kind, step):
        to = wrap(x + step, NX)
        src = (k_hbm, v_hbm, q_hbm)[kind].at[:, columns(to)]
        dst = qb.at[x] if kind == 2 else (kb, vb)[kind].at[z, place(to, step)]
        return remote(src, dst, s1_send.at[kind, step - 1], s1_recv.at[kind, step - 1], at_x(to))

    def first_arrived(kind, step):
        by = wrap(x - step, NX)
        dst = qb.at[by] if kind == 2 else (kb, vb)[kind].at[z, place(x, step)]
        remote(dst, dst, s1_send.at[kind, step - 1], s1_recv.at[kind, step - 1], at_x(by)).wait_recv()

    def toward(side, step):
        return wrap(z - step, NZ) if side == RIGHT else wrap(z + step, NZ)

    def wz_piece(side, owner, step):
        if step < NZ // 2 - 1:
            return wb.at[x, owner]
        return wb.at[x, owner, pl.ds(side * (WCOLS // 2), WCOLS // 2)]

    def wz(side, step):
        piece = wz_piece(side, toward(side, step), step)
        return remote(piece, piece, wz_send.at[side, step], wz_recv.at[side, step], at_z(z_side[side]))

    def wz_arrived(side, step):
        piece = wz_piece(side, toward(side, step + 1), step)
        remote(piece, piece, wz_send.at[side, step], wz_recv.at[side, step], at_z(z_side[side])).wait_recv()

    def kv0(kind, side, at):
        piece, half = (kb, vb)[kind].at[z, at], lax.div(at, 2)
        return remote(
            piece, piece, kv_send.at[kind, side, 0, half], kv_recv.at[kind, side, 0, half], at_z(z_side[side])
        )

    def kv(kind, side, step, half, owner):
        piece = (kb, vb)[kind].at[owner, pl.ds(2 * half, 2)]
        return remote(
            piece, piece, kv_send.at[kind, side, step, half], kv_recv.at[kind, side, step, half],
            at_z(z_side[side]),
        )

    def kv3(kind, side, owner, count):
        piece = (kb, vb)[kind].at[owner, pl.ds(side * count, count)]
        return remote(
            piece, piece, kv_send.at[kind, side, 3, 0], kv_recv.at[kind, side, 3, 0], at_z(z_side[side])
        )

    def turn(at):
        step = lax.div(at + 1, 2)
        return wrap(jnp.where(lax.rem(at, 2) == 1, z - step, z + step), NZ)

    def wx(side, at):
        piece = wb.at[x, turn(at)]
        return remote(piece, piece, wx_send.at[side, at], wx_recv.at[side, at], at_x(x_side[side]))

    def wx_arrived(side, at):
        piece = wb.at[x_side[1 - side], turn(at)]
        remote(piece, piece, wx_send.at[side, at], wx_recv.at[side, at], at_x(x_side[side])).wait_recv()

    def wy_rows(side):
        return pl.ds(0, CUT) if side == RIGHT else pl.ds(CUT, WCOLS - CUT)

    def wy(side, at):
        piece = wb.at[x_side[1 - side], turn(at), wy_rows(side)]
        return remote(piece, piece, wy_send.at[side, at], wy_recv.at[side, at], at_x(x_side[side]))

    def wy_arrived(side, at):
        piece = wb.at[wrap(x + 2, NX), turn(at), wy_rows(side)]
        remote(piece, piece, wy_send.at[side, at], wy_recv.at[side, at], at_x(x_side[side])).wait_recv()

    def spread(at):
        for side in (RIGHT, LEFT):
            wx(side, at).start()

    def hand_on(at):
        for side in (RIGHT, LEFT):
            wx_arrived(side, at)
            wy(side, at).start()

    for kind in (0, 1):
        for step in (1, 3, 2):
            @pl.when(wants(wrap(x + step, NX), x))
            def _():
                first(kind, step).start()
    own[0].wait()
    for side in (RIGHT, LEFT):
        wz(side, 0).start()
    for kind in (0, 1):
        own[1 + kind].wait()
        for side in (RIGHT, LEFT):
            kv0(kind, side, jnp.int32(0)).start()
    for step in (1, 3, 2):
        first(2, step).start()
    spread(jnp.int32(0))

    rows_at = lax.broadcasted_iota(jnp.int32, (128, 128), 0)
    lanes_at = lax.broadcasted_iota(jnp.int32, (128, 128), 1)
    zero = jnp.zeros((128, 128), jnp.float32)
    slot_row = jnp.broadcast_to(slot_ref[...].astype(jnp.float32), (128, 128))
    doc_row = jnp.broadcast_to(doc_ref[...].astype(jnp.float32), (128, 128))
    clip = jnp.sum(jnp.where(rows_at == lanes_at, slot_row, zero), axis=1, keepdims=True)
    clip = jnp.broadcast_to(clip, (128, 128))
    doc = jnp.sum(jnp.where(clip == lanes_at.astype(jnp.float32), doc_row, zero), axis=1, keepdims=True)
    doc = jnp.broadcast_to(doc, (128, 128))
    start = jnp.sum(jnp.where(doc_row < doc, zero + 1.0, zero), axis=1, keepdims=True)
    start = jnp.broadcast_to(start, (128, 128))
    spans = ROWS // SPAN
    wanted = (lax.div(lanes_at, spans) * NZ + z) * spans + lax.rem(lanes_at, spans)
    chosen = rows_at == wanted
    clip_q = jnp.sum(jnp.where(chosen, clip, zero), axis=0, keepdims=True)
    start_q = jnp.sum(jnp.where(chosen, start, zero), axis=0, keepdims=True)
    visible = (clip <= clip_q) & (clip >= start_q)
    seen[...] = jnp.where(visible, zero, zero + MASKED)

    def expand(zz, unused):
        for at in range(NX):
            partner = 2 * lax.div(x, 2) + 1 - lax.rem(x, 2)
            source = wrap(x + (0, -1, 1, 2)[at], NX)
            if at == 1:
                source = jnp.where(full, source, partner)
            for span in range(spans):
                row = seen[pl.ds((source * NZ + zz) * spans + span, 1), :]
                row = jnp.broadcast_to(row, (SPAN, 128)).astype(jnp.bfloat16)
                bias[zz, at, pl.ds(span * SPAN, SPAN), :] = row
        return unused

    lax.fori_loop(0, NZ, expand, 0)
    span_at = lax.div(lax.broadcasted_iota(jnp.int32, (ROWS, 128), 0), SPAN)
    lane_at = lax.broadcasted_iota(jnp.int32, (ROWS, 128), 1)
    for part in range(NX):
        hot[part] = jnp.where(lane_at == span_at + part * spans, 1.0, 0.0).astype(jnp.bfloat16)
    top[...] = jnp.full(top.shape, LOWEST, jnp.float32)
    acc[...] = jnp.zeros(acc.shape, jnp.float32)

    def attend(pairs, parts):
        count = 2 * ROWS

        def join(buf, width):
            return [buf[block, pl.ds(2 * half, 2)].reshape(count, width) for block, half in pairs]

        k_all = jnp.concatenate(
            [jnp.concatenate(both, axis=1) for both in zip(join(kb, HEAD_DIM), join(bias, 128))], axis=0
        )
        ones = jnp.ones((count, 128), jnp.bfloat16)
        v_all = jnp.concatenate([jnp.concatenate([v, ones], axis=1) for v in join(vb, HEAD_DIM)], axis=0)
        count *= len(pairs)
        for part in parts:
            q_all = jnp.concatenate([qb[part], hot[part]], axis=1)
            scores = lax.dot_general(q_all, k_all, NT, preferred_element_type=jnp.float32)
            old = top[part]
            new = jnp.maximum(old, jnp.broadcast_to(jnp.max(scores, axis=1, keepdims=True), old.shape))
            scaled = new * SCALE
            weights = jnp.exp2(scores * SCALE - jnp.concatenate([scaled] * (count // 128), axis=1))
            shrink = jnp.exp2(old * SCALE - scaled)
            fresh = jnp.dot(weights.astype(jnp.bfloat16), v_all, preferred_element_type=jnp.float32)
            acc[part] = acc[part] * jnp.concatenate([shrink, shrink], axis=1) + fresh
            top[part] = new

    def w_step(step):
        for side in (RIGHT, LEFT):
            wz_arrived(side, step)
            wz(side, step + 1).start()
        spread(jnp.int32(2 * step + 1))
        spread(jnp.int32(2 * step + 2))

    def tiles_from(step):
        by = wrap(x - step, NX)

        @pl.when(wants(x, by))
        def _():
            for kind in (0, 1):
                first_arrived(kind, step)
                for side in (RIGHT, LEFT):
                    kv0(kind, side, place(x, step)).start()

    w_step(0)
    tiles_from(1)
    tiles_from(3)
    w_step(1)
    tiles_from(2)
    for step in (1, 3, 2):
        first_arrived(2, step)
    own[3].wait()

    per = jnp.where(full, 2, 4)

    def main(index, unused):
        stage = index - lead
        step, half = lax.div(stage + halves, halves) - 1, lax.rem(stage + halves, halves)
        right, left = wrap(z - step - 1, NZ), wrap(z + step + 1, NZ)

        @pl.when(stage >= 0)
        def _():
            for kind in (0, 1):
                for side, owner in ((RIGHT, right), (LEFT, left)):
                    kv(kind, side, step, half, owner).wait_recv()

                    @pl.when(step < 2)
                    def _():
                        kv(kind, side, step + 1, half, owner).start()

                    @pl.when((step == 2) & full & (half == side))
                    def _():
                        kv3(kind, side, owner, 2).start()

                    @pl.when((step == 2) & not_full)
                    def _():
                        kv3(kind, side, owner, 1).start()

        is_own = stage < 0
        attend(
            (
                (jnp.where(is_own, z, right), jnp.where(is_own, 0, half)),
                (jnp.where(is_own, z, left), jnp.where(is_own, 1, half)),
            ),
            range(NX),
        )

        @pl.when(stage == 0)
        def _():
            w_step(2)

        @pl.when(stage == 1)
        def _():
            for side in (RIGHT, LEFT):
                wz_arrived(side, 3)
            spread(jnp.int32(7))

        def hand(at, unused):
            hand_on(at)
            return unused

        begun = jnp.minimum(per * jnp.maximum(stage - 1, 0), NZ)
        lax.fori_loop(begun, jnp.minimum(per * jnp.maximum(stage, 0), NZ), hand, 0)
        return unused

    lax.fori_loop(0, lead + 3 * halves, main, 0)

    def answer(part):
        return remote(ost.at[part], ob.at[x], o_send.at[part], o_recv.at[x], at_x(part))

    def answer_stat(part):
        return remote(
            stat_out.at[part], stat_in.at[x], stat_send.at[part], stat_recv.at[x], at_x(part)
        )

    eye = rows_at == lanes_at

    def finish(part):
        total = acc[part]
        result = (total[:, :HEAD_DIM] / total[:, HEAD_DIM:]).astype(jnp.bfloat16)
        ost[part] = result

        @pl.when(part != x)
        def _():
            answer(part).start()

        @pl.when(part == x)
        def _():
            ob[x] = result

        @pl.when(not_full)
        def _():
            scaled = top[part] * SCALE
            sums = total[:, HEAD_DIM:]
            rows = []
            for which in (scaled, sums):
                for at in (0, 128):
                    rows.append(jnp.sum(jnp.where(eye, which[at:at + 128], zero), axis=0, keepdims=True))
            stats = jnp.concatenate(rows + [zero[:4]], axis=0)
            stat_out[part] = stats

            @pl.when(part != x)
            def _():
                answer_stat(part).start()

            @pl.when(part == x)
            def _():
                stat_in[x] = stats

    last = wrap(z + NZ // 2, NZ)

    def arrive_last(count):
        for kind in (0, 1):
            for side in (RIGHT, LEFT):
                kv3(kind, side, last, count).wait_recv()

    @pl.when(full)
    def _():
        arrive_last(2)

    @pl.when(not_full)
    def _():
        arrive_last(1)

    def end(pair, unused):
        parts = (2 * pair, 2 * pair + 1)
        attend(((jnp.where(full, last, z), 0), (last, jnp.where(full, 1, 0))), parts)
        for part in parts:
            finish(part)
        return unused

    lax.fori_loop(0, 2, end, 0)

    for giver in range(NX):
        @pl.when(giver != x)
        def _():
            remote(ost.at[0], ob.at[giver], o_send.at[0], o_recv.at[giver], at_x(x_side[0])).wait_recv()

            @pl.when(jnp.logical_not(is_full(giver)))
            def _():
                remote(
                    stat_out.at[0], stat_in.at[giver], stat_send.at[0], stat_recv.at[giver], at_x(x_side[0])
                ).wait_recv()

    def column(stats, first_row):
        parts = []
        for at in (first_row, first_row + 1):
            row = jnp.broadcast_to(stats[at:at + 1], (128, 128))
            whole = jnp.sum(jnp.where(eye, row, zero), axis=1, keepdims=True)
            parts.append(jnp.broadcast_to(whole, (128, 128)))
        return jnp.concatenate(parts, axis=0)

    one, two = 1 - core, 2 + core
    top_one, top_two = column(stat_in[one], 0), column(stat_in[two], 0)
    best = jnp.maximum(top_one, top_two)
    share_one = column(stat_in[one], 2) * jnp.exp2(top_one - best)
    share_two = column(stat_in[two], 2) * jnp.exp2(top_two - best)
    middle = ob[one].astype(jnp.float32) * share_one + ob[two].astype(jnp.float32) * share_two
    middle = (middle / (share_one + share_two)).astype(jnp.bfloat16)
    attn = jnp.concatenate([ob[core], middle, ob[NX - 1 - core]], axis=1)

    pieces = (x, x_side[0], x_side[1], wrap(x + 2, NX))
    owners = [wrap(y + away, NY) for away in (4, 3, -3, 2, -2, 1, -1, 0)]
    cuts = ((0, 1), (1, 2), (3, 5))

    def to_sibling(piece, cut):
        rows = pl.ds(*cuts[cut])
        return remote(
            sib_out.at[piece, rows], sib_in.at[piece, rows],
            sib_send.at[piece, cut], sib_recv.at[piece, cut], sibling,
        )

    def rs(side, step, piece):
        return remote(
            rs_out.at[side, step, piece], rs_in.at[side, step, piece],
            rs_send.at[side, step, piece], rs_recv.at[side, step, piece], at_y(y_side[side]),
        )

    def here(piece, rank):
        return prod[piece, owners[rank], core] + sib_in[piece, rank].astype(jnp.float32)

    def travels(side, step, piece):
        return step > 0 or piece % 2 == side

    def pass_on(side, step, piece):
        total = here(piece, 2 * step - 1 + side if step else 0)
        if step > 0 and travels(side, step - 1, piece):
            rs(side, step - 1, piece).wait_recv()
            total = total + rs_in[side, step - 1, piece].astype(jnp.float32)
        rs_out[side, step, piece] = total.astype(jnp.bfloat16)
        rs(side, step, piece).start()

    def begin(piece):
        to_sibling(piece, 0).wait_recv()
        pass_on(piece % 2, 0, piece)
        to_sibling(piece, 1).wait_recv()
        pass_on(1 - piece % 2, 1, piece)

    for piece in range(NX):
        if piece == NX - 1:
            for side in (RIGHT, LEFT):
                for at in range(NZ):
                    wy_arrived(side, jnp.int32(at))
        part = lax.dot_general(
            attn, wb[pieces[piece]].reshape(PIECE, WROWS), NT, preferred_element_type=jnp.float32
        )
        prod[piece] = part.reshape(NY, 2, MINE, PIECE)
        for rank in range(NY):
            sib_out[piece, rank] = prod[piece, owners[rank], 1 - core].astype(jnp.bfloat16)
            if rank in (0, 2):
                to_sibling(piece, rank // 2).start()
        if piece:
            begin(piece - 1)
    for piece in range(NX):
        to_sibling(piece, 2).start()
    begin(NX - 1)
    late = ((1, 3, 0, 2), (0, 2, 1, 3))
    for at in (2, 3):
        for side in (RIGHT, LEFT):
            pass_on(side, 1, late[side][at])
    for piece in range(NX):
        to_sibling(piece, 2).wait_recv()
    for step in range(2, NY // 2):
        for at in range(NX):
            for side in (RIGHT, LEFT):
                pass_on(side, step, late[side][at])
    for piece in (1, 0, 3, 2):
        total = here(piece, NY - 1)
        for side in (RIGHT, LEFT):
            rs(side, NY // 2 - 1, piece).wait_recv()
            total = total + rs_in[side, NY // 2 - 1, piece].astype(jnp.float32)
        out_ref[:, pl.ds(pl.multiple_of(pieces[piece] * PIECE, PIECE), PIECE)] = total.astype(jnp.bfloat16)

    for step in (1, 2, 3):
        first(2, step).wait_send()

        @pl.when(wants(wrap(x + step, NX), x))
        def _():
            for kind in (0, 1):
                first(kind, step).wait_send()

    def sent(half, unused):
        for kind in (0, 1):
            for side in (RIGHT, LEFT):
                for step in (0, 1, 2):
                    kv(kind, side, step, half, z).wait_send()
        return unused

    lax.fori_loop(0, halves, sent, 0)
    for kind in (0, 1):
        for side in (RIGHT, LEFT):
            @pl.when(full)
            def _():
                kv3(kind, side, z, 2).wait_send()

            @pl.when(not_full)
            def _():
                kv3(kind, side, z, 1).wait_send()
    for side in (RIGHT, LEFT):
        for step in range(NZ // 2):
            wz(side, step).wait_send()
        for at in range(NZ):
            wx(side, jnp.int32(at)).wait_send()
            wy(side, jnp.int32(at)).wait_send()
    for part in range(NX):
        @pl.when(part != x)
        def _():
            answer(part).wait_send()

            @pl.when(not_full)
            def _():
                answer_stat(part).wait_send()
    for piece in range(NX):
        for cut in range(3):
            to_sibling(piece, cut).wait_send()
    for step in range(NY // 2):
        for piece in range(NX):
            for side in (RIGHT, LEFT):
                if travels(side, step, piece):
                    rs(side, step, piece).wait_send()


def local(query, keys, values, span_slot, span_doc, w_out):
    whole = pl.BlockSpec(memory_space=pltpu.VMEM)
    remote = pl.BlockSpec(memory_space=pl.ANY)
    bf16, f32 = jnp.bfloat16, jnp.float32
    dma = pltpu.SemaphoreType.DMA
    return pl.pallas_call(
        kernel,
        out_shape=jax.ShapeDtypeStruct((MINE, D), bf16),
        in_specs=[remote] * 4 + [whole] * 2,
        out_specs=whole,
        scratch_shapes=[
            pltpu.VMEM((NX, ROWS, HEAD_DIM), bf16),
            pltpu.VMEM((NX, ROWS, 128), bf16),
            pltpu.VMEM((NZ, NX, ROWS, HEAD_DIM), bf16),
            pltpu.VMEM((NZ, NX, ROWS, HEAD_DIM), bf16),
            pltpu.VMEM((128, 128), f32),
            pltpu.VMEM((NZ, NX, ROWS, 128), bf16),
            pltpu.VMEM((NX, NZ, WCOLS, WROWS), bf16),
            pltpu.VMEM((NX, ROWS, 128), f32),
            pltpu.VMEM((NX, ROWS, 256), f32),
            pltpu.VMEM((NX, ROWS, HEAD_DIM), bf16),
            pltpu.VMEM((NX, ROWS, HEAD_DIM), bf16),
            pltpu.VMEM((NX, 8, 128), f32),
            pltpu.VMEM((NX, 8, 128), f32),
            pltpu.VMEM((NX, NY, 2, MINE, PIECE), f32),
            pltpu.VMEM((NX, NY, MINE, PIECE), bf16),
            pltpu.VMEM((NX, NY, MINE, PIECE), bf16),
            pltpu.VMEM((2, NY // 2, NX, MINE, PIECE), bf16),
            pltpu.VMEM((2, NY // 2, NX, MINE, PIECE), bf16),
            dma((4,)),
            dma((3, 3)), dma((3, 3)),
            dma((2, 2, 4, 2)), dma((2, 2, 4, 2)),
            dma((2, NZ // 2)), dma((2, NZ // 2)),
            dma((2, NZ)), dma((2, NZ)),
            dma((2, NZ)), dma((2, NZ)),
            dma((NX,)), dma((NX,)),
            dma((NX,)), dma((NX,)),
            dma((NX, 3)), dma((NX, 3)),
            dma((2, NY // 2, NX)), dma((2, NY // 2, NX)),
        ],
        compiler_params=pltpu.CompilerParams(
            collective_id=0, has_side_effects=True, vmem_limit_bytes=56 << 20
        ),
        cost_estimate=pl.CostEstimate(
            flops=2 * BLOCK * 8192 * 512 + 2 * ROWS * WROWS * D,
            bytes_accessed=1 << 21, transcendentals=BLOCK * 8192,
        ),
    )(query, keys, values, w_out.T, span_slot.reshape(1, 128), span_doc.reshape(1, 128))


def solution(mesh):
    placed = (P("ctx", "head"), P("ctx", "head"), P("ctx", "head"), P(), P(), P("head", "ctx"))
    return jax.shard_map(
        local, mesh=mesh, in_specs=placed, out_specs=P(("ctx", "head"), None), check_vma=False
    )
```

```python
import math

import jax
import jax.numpy as jnp
from jax import lax
from jax.experimental import pallas as pl
from jax.experimental.pallas import tpu as pltpu
from jax.sharding import PartitionSpec as P

HEAD_DIM = 128
SPAN = 64
NX, NZ, NY = 4, 8, 8
ROWS = 256
HELD = 3
BLOCK = NX * ROWS
WCOLS = 192
WROWS = HELD * HEAD_DIM
PIECE = NZ * WCOLS
D = NX * PIECE
MINE = 16
MASKED = -1e30
LOWEST = -2e30
CUT = 96
EARLY = 4
SCALE = math.log2(math.e) / math.sqrt(HEAD_DIM)
MESH = pl.DeviceIdType.MESH
RIGHT, LEFT = 0, 1
NT = (((1,), (1,)), ((), ()))


def wrap(value, size):
    return lax.rem(value + 2 * size, size)


def kernel(
    q_hbm, k_hbm, v_hbm, w_hbm, slot_ref, doc_ref, out_ref,
    qb, hot, kb, vb, seen, bias, wb, top, acc, ost, ob, stat_out, stat_in,
    prod, sib_out, sib_in, rs_out, rs_in,
    own_sem, s1_send, s1_recv, kv_send, kv_recv, wz_send, wz_recv,
    wx_send, wx_recv, wy_send, wy_recv, o_send, o_recv, stat_send, stat_recv,
    sib_send, sib_recv, rs_send, rs_recv,
):
    ctx, head = lax.axis_index("ctx"), lax.axis_index("head")
    x, z = lax.div(ctx, NZ), lax.rem(ctx, NZ)
    y, core = lax.div(head, 2), lax.rem(head, 2)

    def at_x(to):
        return (to * NZ + z, head)

    def at_z(to):
        return (x * NZ + to, head)

    def at_y(to):
        return (ctx, to * 2 + core)

    sibling = (ctx, y * 2 + 1 - core)
    z_side = (wrap(z + 1, NZ), wrap(z - 1, NZ))
    x_side = (wrap(x + 1, NX), wrap(x - 1, NX))
    y_side = (wrap(y + 1, NY), wrap(y - 1, NY))

    def remote(src, dst, send, recv, device):
        return pltpu.make_async_remote_copy(
            src_ref=src, dst_ref=dst, send_sem=send, recv_sem=recv,
            device_id=device, device_id_type=MESH,
        )

    def is_full(ring):
        edge = jnp.where((ring == 0) | (ring == NX - 1), 1, 0)
        return edge + core == 1

    def head_of(ring):
        return jnp.where(is_full(ring), 2 * lax.div(ring, 2), 1)

    def columns(ring):
        return pl.ds(pl.multiple_of(head_of(ring) * HEAD_DIM, HEAD_DIM), HEAD_DIM)

    def place(ring, step):
        return jnp.where(is_full(ring), (1, 3, 2)[step - 1], 1)

    def wants(ring, source):
        return is_full(ring) | (lax.div(ring, 2) == lax.div(source, 2))

    full = is_full(x)
    not_full = jnp.logical_not(full)
    halves = jnp.where(full, 2, 1)
    lead = jnp.where(full, 1, 0)

    own = [
        pltpu.make_async_copy(w_hbm, wb.at[x, z], own_sem.at[0]),
        pltpu.make_async_copy(k_hbm.at[:, columns(x)], kb.at[z, 0], own_sem.at[1]),
        pltpu.make_async_copy(v_hbm.at[:, columns(x)], vb.at[z, 0], own_sem.at[2]),
        pltpu.make_async_copy(q_hbm.at[:, columns(x)], qb.at[x], own_sem.at[3]),
    ]
    for copy in own:
        copy.start()

    barrier = pltpu.get_barrier_semaphore()
    peers = [at_x(wrap(x + step, NX)) for step in (1, 2, 3)]
    peers += [at_z(z_side[0]), at_z(z_side[1]), at_y(y_side[0]), at_y(y_side[1]), sibling]
    for peer in peers:
        pl.semaphore_signal(barrier, inc=1, device_id=peer, device_id_type=MESH)
    pl.semaphore_wait(barrier, len(peers))

    def first(kind, step):
        to = wrap(x + step, NX)
        src = (k_hbm, v_hbm, q_hbm)[kind].at[:, columns(to)]
        dst = qb.at[x] if kind == 2 else (kb, vb)[kind].at[z, place(to, step)]
        return remote(src, dst, s1_send.at[kind, step - 1], s1_recv.at[kind, step - 1], at_x(to))

    def first_arrived(kind, step):
        by = wrap(x - step, NX)
        dst = qb.at[by] if kind == 2 else (kb, vb)[kind].at[z, place(x, step)]
        remote(dst, dst, s1_send.at[kind, step - 1], s1_recv.at[kind, step - 1], at_x(by)).wait_recv()

    def toward(side, step):
        return wrap(z - step, NZ) if side == RIGHT else wrap(z + step, NZ)

    def wz_piece(side, owner, step):
        if step < NZ // 2 - 1:
            return wb.at[x, owner]
        return wb.at[x, owner, pl.ds(side * (WCOLS // 2), WCOLS // 2)]

    def wz(side, step):
        piece = wz_piece(side, toward(side, step), step)
        return remote(piece, piece, wz_send.at[side, step], wz_recv.at[side, step], at_z(z_side[side]))

    def wz_arrived(side, step):
        piece = wz_piece(side, toward(side, step + 1), step)
        remote(piece, piece, wz_send.at[side, step], wz_recv.at[side, step], at_z(z_side[side])).wait_recv()

    def kv0(kind, side, at):
        piece, half = (kb, vb)[kind].at[z, at], lax.div(at, 2)
        return remote(
            piece, piece, kv_send.at[kind, side, 0, half], kv_recv.at[kind, side, 0, half], at_z(z_side[side])
        )

    def kv(kind, side, step, half, owner):
        piece = (kb, vb)[kind].at[owner, pl.ds(2 * half, 2)]
        return remote(
            piece, piece, kv_send.at[kind, side, step, half], kv_recv.at[kind, side, step, half],
            at_z(z_side[side]),
        )

    def kv3(kind, side, owner, count):
        piece = (kb, vb)[kind].at[owner, pl.ds(side * count, count)]
        return remote(
            piece, piece, kv_send.at[kind, side, 3, 0], kv_recv.at[kind, side, 3, 0], at_z(z_side[side])
        )

    def turn(at):
        step = lax.div(at + 1, 2)
        return wrap(jnp.where(lax.rem(at, 2) == 1, z - step, z + step), NZ)

    def wx(side, at):
        piece = wb.at[x, turn(at)]
        return remote(piece, piece, wx_send.at[side, at], wx_recv.at[side, at], at_x(x_side[side]))

    def wx_arrived(side, at):
        piece = wb.at[x_side[1 - side], turn(at)]
        remote(piece, piece, wx_send.at[side, at], wx_recv.at[side, at], at_x(x_side[side])).wait_recv()

    def wy_rows(side):
        return pl.ds(0, CUT) if side == RIGHT else pl.ds(CUT, WCOLS - CUT)

    def wy(side, at):
        piece = wb.at[x_side[1 - side], turn(at), wy_rows(side)]
        return remote(piece, piece, wy_send.at[side, at], wy_recv.at[side, at], at_x(x_side[side]))

    def wy_arrived(side, at):
        piece = wb.at[wrap(x + 2, NX), turn(at), wy_rows(side)]
        remote(piece, piece, wy_send.at[side, at], wy_recv.at[side, at], at_x(x_side[side])).wait_recv()

    def spread(at):
        for side in (RIGHT, LEFT):
            wx(side, at).start()

    def hand_on(at):
        for side in (RIGHT, LEFT):
            wx_arrived(side, at)
            wy(side, at).start()

    for kind in (0, 1):
        for step in (1, 3, 2):
            @pl.when(wants(wrap(x + step, NX), x))
            def _():
                first(kind, step).start()
    own[0].wait()
    for side in (RIGHT, LEFT):
        wz(side, 0).start()
    for kind in (0, 1):
        own[1 + kind].wait()
        for side in (RIGHT, LEFT):
            kv0(kind, side, jnp.int32(0)).start()
    for step in (1, 3, 2):
        first(2, step).start()
    spread(jnp.int32(0))

    rows_at = lax.broadcasted_iota(jnp.int32, (128, 128), 0)
    lanes_at = lax.broadcasted_iota(jnp.int32, (128, 128), 1)
    zero = jnp.zeros((128, 128), jnp.float32)
    slot_row = jnp.broadcast_to(slot_ref[...].astype(jnp.float32), (128, 128))
    doc_row = jnp.broadcast_to(doc_ref[...].astype(jnp.float32), (128, 128))
    clip = jnp.sum(jnp.where(rows_at == lanes_at, slot_row, zero), axis=1, keepdims=True)
    clip = jnp.broadcast_to(clip, (128, 128))
    doc = jnp.sum(jnp.where(clip == lanes_at.astype(jnp.float32), doc_row, zero), axis=1, keepdims=True)
    doc = jnp.broadcast_to(doc, (128, 128))
    start = jnp.sum(jnp.where(doc_row < doc, zero + 1.0, zero), axis=1, keepdims=True)
    start = jnp.broadcast_to(start, (128, 128))
    spans = ROWS // SPAN
    wanted = (lax.div(lanes_at, spans) * NZ + z) * spans + lax.rem(lanes_at, spans)
    chosen = rows_at == wanted
    clip_q = jnp.sum(jnp.where(chosen, clip, zero), axis=0, keepdims=True)
    start_q = jnp.sum(jnp.where(chosen, start, zero), axis=0, keepdims=True)
    visible = (clip <= clip_q) & (clip >= start_q)
    seen[...] = jnp.where(visible, zero, zero + MASKED)

    def expand(zz, unused):
        for at in range(NX):
            partner = 2 * lax.div(x, 2) + 1 - lax.rem(x, 2)
            source = wrap(x + (0, -1, 1, 2)[at], NX)
            if at == 1:
                source = jnp.where(full, source, partner)
            for span in range(spans):
                row = seen[pl.ds((source * NZ + zz) * spans + span, 1), :]
                row = jnp.broadcast_to(row, (SPAN, 128)).astype(jnp.bfloat16)
                bias[zz, at, pl.ds(span * SPAN, SPAN), :] = row
        return unused

    lax.fori_loop(0, NZ, expand, 0)
    span_at = lax.div(lax.broadcasted_iota(jnp.int32, (ROWS, 128), 0), SPAN)
    lane_at = lax.broadcasted_iota(jnp.int32, (ROWS, 128), 1)
    for part in range(NX):
        hot[part] = jnp.where(lane_at == span_at + part * spans, 1.0, 0.0).astype(jnp.bfloat16)
    top[...] = jnp.full(top.shape, LOWEST, jnp.float32)
    acc[...] = jnp.zeros(acc.shape, jnp.float32)

    def attend(pairs, parts):
        count = 2 * ROWS

        def join(buf, width):
            return [buf[block, pl.ds(2 * half, 2)].reshape(count, width) for block, half in pairs]

        k_all = jnp.concatenate(
            [jnp.concatenate(both, axis=1) for both in zip(join(kb, HEAD_DIM), join(bias, 128))], axis=0
        )
        ones = jnp.ones((count, 128), jnp.bfloat16)
        v_all = jnp.concatenate([jnp.concatenate([v, ones], axis=1) for v in join(vb, HEAD_DIM)], axis=0)
        count *= len(pairs)
        for part in parts:
            q_all = jnp.concatenate([qb[part], hot[part]], axis=1)
            scores = lax.dot_general(q_all, k_all, NT, preferred_element_type=jnp.float32)
            old = top[part]
            new = jnp.maximum(old, jnp.broadcast_to(jnp.max(scores, axis=1, keepdims=True), old.shape))
            scaled = new * SCALE
            weights = jnp.exp2(scores * SCALE - jnp.concatenate([scaled] * (count // 128), axis=1))
            shrink = jnp.exp2(old * SCALE - scaled)
            fresh = jnp.dot(weights.astype(jnp.bfloat16), v_all, preferred_element_type=jnp.float32)
            acc[part] = acc[part] * jnp.concatenate([shrink, shrink], axis=1) + fresh
            top[part] = new

    def w_step(step):
        for side in (RIGHT, LEFT):
            wz_arrived(side, step)
            wz(side, step + 1).start()
        spread(jnp.int32(2 * step + 1))
        spread(jnp.int32(2 * step + 2))

    def tiles_from(step):
        by = wrap(x - step, NX)

        @pl.when(wants(x, by))
        def _():
            for kind in (0, 1):
                first_arrived(kind, step)
                for side in (RIGHT, LEFT):
                    kv0(kind, side, place(x, step)).start()

    w_step(0)
    tiles_from(1)
    tiles_from(3)
    w_step(1)
    tiles_from(2)
    for step in (1, 3, 2):
        first_arrived(2, step)
    own[3].wait()

    per = jnp.where(full, 1, 2)

    def main(index, unused):
        stage = index - lead
        step, half = lax.div(stage + halves, halves) - 1, lax.rem(stage + halves, halves)
        right, left = wrap(z - step - 1, NZ), wrap(z + step + 1, NZ)

        @pl.when(stage >= 0)
        def _():
            for kind in (0, 1):
                for side, owner in ((RIGHT, right), (LEFT, left)):
                    kv(kind, side, step, half, owner).wait_recv()

                    @pl.when(step < 2)
                    def _():
                        kv(kind, side, step + 1, half, owner).start()

                    @pl.when((step == 2) & full & (half == side))
                    def _():
                        kv3(kind, side, owner, 2).start()

                    @pl.when((step == 2) & not_full)
                    def _():
                        kv3(kind, side, owner, 1).start()

        is_own = stage < 0
        attend(
            (
                (jnp.where(is_own, z, right), jnp.where(is_own, 0, half)),
                (jnp.where(is_own, z, left), jnp.where(is_own, 1, half)),
            ),
            range(NX),
        )

        @pl.when(stage == 0)
        def _():
            w_step(2)

        @pl.when(stage == 1)
        def _():
            for side in (RIGHT, LEFT):
                wz_arrived(side, 3)
            spread(jnp.int32(7))

        def hand(at, unused):
            hand_on(at)
            return unused

        begun = jnp.minimum(per * jnp.maximum(stage - 1, 0), EARLY)
        lax.fori_loop(begun, jnp.minimum(per * jnp.maximum(stage, 0), EARLY), hand, 0)
        return unused

    lax.fori_loop(0, lead + 3 * halves, main, 0)

    def answer(part):
        return remote(ost.at[part], ob.at[x], o_send.at[part], o_recv.at[x], at_x(part))

    def answer_stat(part):
        return remote(
            stat_out.at[part], stat_in.at[x], stat_send.at[part], stat_recv.at[x], at_x(part)
        )

    eye = rows_at == lanes_at

    def finish(part):
        total = acc[part]
        result = (total[:, :HEAD_DIM] / total[:, HEAD_DIM:]).astype(jnp.bfloat16)
        ost[part] = result

        @pl.when(part != x)
        def _():
            answer(part).start()

        @pl.when(part == x)
        def _():
            ob[x] = result

        @pl.when(not_full)
        def _():
            scaled = top[part] * SCALE
            sums = total[:, HEAD_DIM:]
            rows = []
            for which in (scaled, sums):
                for at in (0, 128):
                    rows.append(jnp.sum(jnp.where(eye, which[at:at + 128], zero), axis=0, keepdims=True))
            stats = jnp.concatenate(rows + [zero[:4]], axis=0)
            stat_out[part] = stats

            @pl.when(part != x)
            def _():
                answer_stat(part).start()

            @pl.when(part == x)
            def _():
                stat_in[x] = stats

    last = wrap(z + NZ // 2, NZ)

    def arrive_last(count):
        for kind in (0, 1):
            for side in (RIGHT, LEFT):
                kv3(kind, side, last, count).wait_recv()

    @pl.when(full)
    def _():
        arrive_last(2)

    @pl.when(not_full)
    def _():
        arrive_last(1)

    def end(pair, unused):
        parts = (2 * pair, 2 * pair + 1)
        attend(((jnp.where(full, last, z), 0), (last, jnp.where(full, 1, 0))), parts)
        for part in parts:
            finish(part)
        return unused

    lax.fori_loop(0, 2, end, 0)

    for at in range(EARLY, NZ):
        hand_on(jnp.int32(at))


    for giver in range(NX):
        @pl.when(giver != x)
        def _():
            remote(ost.at[0], ob.at[giver], o_send.at[0], o_recv.at[giver], at_x(x_side[0])).wait_recv()

            @pl.when(jnp.logical_not(is_full(giver)))
            def _():
                remote(
                    stat_out.at[0], stat_in.at[giver], stat_send.at[0], stat_recv.at[giver], at_x(x_side[0])
                ).wait_recv()

    def column(stats, first_row):
        parts = []
        for at in (first_row, first_row + 1):
            row = jnp.broadcast_to(stats[at:at + 1], (128, 128))
            whole = jnp.sum(jnp.where(eye, row, zero), axis=1, keepdims=True)
            parts.append(jnp.broadcast_to(whole, (128, 128)))
        return jnp.concatenate(parts, axis=0)

    one, two = 1 - core, 2 + core
    top_one, top_two = column(stat_in[one], 0), column(stat_in[two], 0)
    best = jnp.maximum(top_one, top_two)
    share_one = column(stat_in[one], 2) * jnp.exp2(top_one - best)
    share_two = column(stat_in[two], 2) * jnp.exp2(top_two - best)
    middle = ob[one].astype(jnp.float32) * share_one + ob[two].astype(jnp.float32) * share_two
    middle = (middle / (share_one + share_two)).astype(jnp.bfloat16)
    attn = jnp.concatenate([ob[core], middle, ob[NX - 1 - core]], axis=1)

    pieces = (x, x_side[0], x_side[1], wrap(x + 2, NX))
    owners = [wrap(y + away, NY) for away in (4, 3, -3, 2, -2, 1, -1, 0)]
    cuts = ((0, 1), (1, 2), (3, 5))

    def to_sibling(piece, cut):
        rows = pl.ds(*cuts[cut])
        return remote(
            sib_out.at[piece, rows], sib_in.at[piece, rows],
            sib_send.at[piece, cut], sib_recv.at[piece, cut], sibling,
        )

    def rs(side, step, piece):
        return remote(
            rs_out.at[side, step, piece], rs_in.at[side, step, piece],
            rs_send.at[side, step, piece], rs_recv.at[side, step, piece], at_y(y_side[side]),
        )

    def here(piece, rank):
        return prod[piece, owners[rank], core] + sib_in[piece, rank].astype(jnp.float32)

    def travels(side, step, piece):
        return step > 0 or piece % 2 == side

    def pass_on(side, step, piece):
        total = here(piece, 2 * step - 1 + side if step else 0)
        if step > 0 and travels(side, step - 1, piece):
            rs(side, step - 1, piece).wait_recv()
            total = total + rs_in[side, step - 1, piece].astype(jnp.float32)
        rs_out[side, step, piece] = total.astype(jnp.bfloat16)
        rs(side, step, piece).start()

    def begin(piece):
        to_sibling(piece, 0).wait_recv()
        pass_on(piece % 2, 0, piece)
        to_sibling(piece, 1).wait_recv()
        pass_on(1 - piece % 2, 1, piece)

    for piece in range(NX):
        if piece == NX - 1:
            begin(NX - 2)
            for side in (RIGHT, LEFT):
                for at in range(NZ):
                    wy_arrived(side, jnp.int32(at))
        part = lax.dot_general(
            attn, wb[pieces[piece]].reshape(PIECE, WROWS), NT, preferred_element_type=jnp.float32
        )
        prod[piece] = part.reshape(NY, 2, MINE, PIECE)
        for rank in range(NY):
            sib_out[piece, rank] = prod[piece, owners[rank], 1 - core].astype(jnp.bfloat16)
            if rank in (0, 2):
                to_sibling(piece, rank // 2).start()
        if piece in (1, 2):
            begin(piece - 1)
    for piece in range(NX):
        to_sibling(piece, 2).start()
    begin(NX - 1)
    late = ((1, 3, 0, 2), (0, 2, 1, 3))
    for at in (2, 3):
        for side in (RIGHT, LEFT):
            pass_on(side, 1, late[side][at])
    for piece in range(NX):
        to_sibling(piece, 2).wait_recv()
    for step in range(2, NY // 2):
        for at in range(NX):
            for side in (RIGHT, LEFT):
                pass_on(side, step, late[side][at])
    for step in (1, 2, 3):
        first(2, step).wait_send()

        @pl.when(wants(wrap(x + step, NX), x))
        def _():
            for kind in (0, 1):
                first(kind, step).wait_send()

    def sent(half, unused):
        for kind in (0, 1):
            for side in (RIGHT, LEFT):
                for step in (0, 1, 2):
                    kv(kind, side, step, half, z).wait_send()
        return unused

    lax.fori_loop(0, halves, sent, 0)
    for kind in (0, 1):
        for side in (RIGHT, LEFT):
            @pl.when(full)
            def _():
                kv3(kind, side, z, 2).wait_send()

            @pl.when(not_full)
            def _():
                kv3(kind, side, z, 1).wait_send()
    for side in (RIGHT, LEFT):
        for step in range(NZ // 2):
            wz(side, step).wait_send()
        for at in range(NZ):
            wx(side, jnp.int32(at)).wait_send()
            wy(side, jnp.int32(at)).wait_send()
    for part in range(NX):
        @pl.when(part != x)
        def _():
            answer(part).wait_send()

            @pl.when(not_full)
            def _():
                answer_stat(part).wait_send()
    for piece in range(NX):
        for cut in range(3):
            to_sibling(piece, cut).wait_send()
    for step in range(NY // 2 - 1):
        for piece in range(NX):
            for side in (RIGHT, LEFT):
                if travels(side, step, piece):
                    rs(side, step, piece).wait_send()

    for piece in (1, 0, 3, 2):
        total = here(piece, NY - 1)
        for side in (RIGHT, LEFT):
            rs(side, NY // 2 - 1, piece).wait_recv()
            total = total + rs_in[side, NY // 2 - 1, piece].astype(jnp.float32)
        out_ref[:, pl.ds(pl.multiple_of(pieces[piece] * PIECE, PIECE), PIECE)] = total.astype(jnp.bfloat16)
    for piece in range(NX):
        for side in (RIGHT, LEFT):
            rs(side, NY // 2 - 1, piece).wait_send()


def local(query, keys, values, span_slot, span_doc, w_out):
    whole = pl.BlockSpec(memory_space=pltpu.VMEM)
    remote = pl.BlockSpec(memory_space=pl.ANY)
    bf16, f32 = jnp.bfloat16, jnp.float32
    dma = pltpu.SemaphoreType.DMA
    return pl.pallas_call(
        kernel,
        out_shape=jax.ShapeDtypeStruct((MINE, D), bf16),
        in_specs=[remote] * 4 + [whole] * 2,
        out_specs=whole,
        scratch_shapes=[
            pltpu.VMEM((NX, ROWS, HEAD_DIM), bf16),
            pltpu.VMEM((NX, ROWS, 128), bf16),
            pltpu.VMEM((NZ, NX, ROWS, HEAD_DIM), bf16),
            pltpu.VMEM((NZ, NX, ROWS, HEAD_DIM), bf16),
            pltpu.VMEM((128, 128), f32),
            pltpu.VMEM((NZ, NX, ROWS, 128), bf16),
            pltpu.VMEM((NX, NZ, WCOLS, WROWS), bf16),
            pltpu.VMEM((NX, ROWS, 128), f32),
            pltpu.VMEM((NX, ROWS, 256), f32),
            pltpu.VMEM((NX, ROWS, HEAD_DIM), bf16),
            pltpu.VMEM((NX, ROWS, HEAD_DIM), bf16),
            pltpu.VMEM((NX, 8, 128), f32),
            pltpu.VMEM((NX, 8, 128), f32),
            pltpu.VMEM((NX, NY, 2, MINE, PIECE), f32),
            pltpu.VMEM((NX, NY, MINE, PIECE), bf16),
            pltpu.VMEM((NX, NY, MINE, PIECE), bf16),
            pltpu.VMEM((2, NY // 2, NX, MINE, PIECE), bf16),
            pltpu.VMEM((2, NY // 2, NX, MINE, PIECE), bf16),
            dma((4,)),
            dma((3, 3)), dma((3, 3)),
            dma((2, 2, 4, 2)), dma((2, 2, 4, 2)),
            dma((2, NZ // 2)), dma((2, NZ // 2)),
            dma((2, NZ)), dma((2, NZ)),
            dma((2, NZ)), dma((2, NZ)),
            dma((NX,)), dma((NX,)),
            dma((NX,)), dma((NX,)),
            dma((NX, 3)), dma((NX, 3)),
            dma((2, NY // 2, NX)), dma((2, NY // 2, NX)),
        ],
        compiler_params=pltpu.CompilerParams(
            collective_id=0, has_side_effects=True, vmem_limit_bytes=56 << 20
        ),
        cost_estimate=pl.CostEstimate(
            flops=2 * BLOCK * 8192 * 512 + 2 * ROWS * WROWS * D,
            bytes_accessed=1 << 21, transcendentals=BLOCK * 8192,
        ),
    )(query, keys, values, w_out.T, span_slot.reshape(1, 128), span_doc.reshape(1, 128))


def solution(mesh):
    placed = (P("ctx", "head"), P("ctx", "head"), P("ctx", "head"), P(), P(), P("head", "ctx"))
    return jax.shard_map(
        local, mesh=mesh, in_specs=placed, out_specs=P(("ctx", "head"), None), check_vma=False
    )
```

```python
import math

import jax
import jax.numpy as jnp
from jax import lax
from jax.experimental import pallas as pl
from jax.experimental.pallas import tpu as pltpu
from jax.sharding import PartitionSpec as P

HEAD_DIM = 128
SPAN = 64
NX, NZ, NY = 4, 8, 8
ROWS = 256
HELD = 3
BLOCK = NX * ROWS
WCOLS = 192
WROWS = HELD * HEAD_DIM
PIECE = NZ * WCOLS
D = NX * PIECE
MINE = 16
MASKED = -1e30
LOWEST = -2e30
CUT = 96
EARLY = 4
SCALE = math.log2(math.e) / math.sqrt(HEAD_DIM)
MESH = pl.DeviceIdType.MESH
RIGHT, LEFT = 0, 1
NT = (((1,), (1,)), ((), ()))


def wrap(value, size):
    return lax.rem(value + 2 * size, size)


def kernel(
    q_hbm, k_hbm, v_hbm, w_hbm, slot_ref, doc_ref, out_ref,
    qb, hot, kb, vb, seen, bias, wb, top, acc, ost, ob, stat_out, stat_in,
    prod, sib_out, sib_in, rs_out, rs_in,
    own_sem, s1_send, s1_recv, kv_send, kv_recv, wz_send, wz_recv,
    wx_send, wx_recv, wy_send, wy_recv, o_send, o_recv, stat_send, stat_recv,
    sib_send, sib_recv, rs_send, rs_recv,
):
    ctx, head = lax.axis_index("ctx"), lax.axis_index("head")
    x, z = lax.div(ctx, NZ), lax.rem(ctx, NZ)
    y, core = lax.div(head, 2), lax.rem(head, 2)

    def at_x(to):
        return (to * NZ + z, head)

    def at_z(to):
        return (x * NZ + to, head)

    def at_y(to):
        return (ctx, to * 2 + core)

    sibling = (ctx, y * 2 + 1 - core)
    z_side = (wrap(z + 1, NZ), wrap(z - 1, NZ))
    x_side = (wrap(x + 1, NX), wrap(x - 1, NX))
    y_side = (wrap(y + 1, NY), wrap(y - 1, NY))

    def remote(src, dst, send, recv, device):
        return pltpu.make_async_remote_copy(
            src_ref=src, dst_ref=dst, send_sem=send, recv_sem=recv,
            device_id=device, device_id_type=MESH,
        )

    def is_full(ring):
        edge = jnp.where((ring == 0) | (ring == NX - 1), 1, 0)
        return edge + core == 1

    def head_of(ring):
        return jnp.where(is_full(ring), 2 * lax.div(ring, 2), 1)

    def columns(ring):
        return pl.ds(pl.multiple_of(head_of(ring) * HEAD_DIM, HEAD_DIM), HEAD_DIM)

    def place(ring, step):
        return jnp.where(is_full(ring), (1, 3, 2)[step - 1], 1)

    def wants(ring, source):
        return is_full(ring) | (lax.div(ring, 2) == lax.div(source, 2))

    full = is_full(x)
    not_full = jnp.logical_not(full)
    halves = jnp.where(full, 2, 1)
    lead = jnp.where(full, 1, 0)

    own = [
        pltpu.make_async_copy(w_hbm, wb.at[x, z], own_sem.at[0]),
        pltpu.make_async_copy(k_hbm.at[:, columns(x)], kb.at[z, 0], own_sem.at[1]),
        pltpu.make_async_copy(v_hbm.at[:, columns(x)], vb.at[z, 0], own_sem.at[2]),
        pltpu.make_async_copy(q_hbm.at[:, columns(x)], qb.at[x], own_sem.at[3]),
    ]
    for copy in own:
        copy.start()

    barrier = pltpu.get_barrier_semaphore()
    peers = [at_x(wrap(x + step, NX)) for step in (1, 2, 3)]
    peers += [at_z(z_side[0]), at_z(z_side[1]), at_y(y_side[0]), at_y(y_side[1]), sibling]
    for peer in peers:
        pl.semaphore_signal(barrier, inc=1, device_id=peer, device_id_type=MESH)
    pl.semaphore_wait(barrier, len(peers))

    def first(kind, step):
        to = wrap(x + step, NX)
        src = (k_hbm, v_hbm, q_hbm)[kind].at[:, columns(to)]
        dst = qb.at[x] if kind == 2 else (kb, vb)[kind].at[z, place(to, step)]
        return remote(src, dst, s1_send.at[kind, step - 1], s1_recv.at[kind, step - 1], at_x(to))

    def first_arrived(kind, step):
        by = wrap(x - step, NX)
        dst = qb.at[by] if kind == 2 else (kb, vb)[kind].at[z, place(x, step)]
        remote(dst, dst, s1_send.at[kind, step - 1], s1_recv.at[kind, step - 1], at_x(by)).wait_recv()

    def toward(side, step):
        return wrap(z - step, NZ) if side == RIGHT else wrap(z + step, NZ)

    def wz_piece(side, owner, step):
        if step < NZ // 2 - 1:
            return wb.at[x, owner]
        return wb.at[x, owner, pl.ds(side * (WCOLS // 2), WCOLS // 2)]

    def wz(side, step):
        piece = wz_piece(side, toward(side, step), step)
        return remote(piece, piece, wz_send.at[side, step], wz_recv.at[side, step], at_z(z_side[side]))

    def wz_arrived(side, step):
        piece = wz_piece(side, toward(side, step + 1), step)
        remote(piece, piece, wz_send.at[side, step], wz_recv.at[side, step], at_z(z_side[side])).wait_recv()

    def kv0(kind, side, at):
        piece, half = (kb, vb)[kind].at[z, at], lax.div(at, 2)
        return remote(
            piece, piece, kv_send.at[kind, side, 0, half], kv_recv.at[kind, side, 0, half], at_z(z_side[side])
        )

    def kv(kind, side, step, half, owner):
        piece = (kb, vb)[kind].at[owner, pl.ds(2 * half, 2)]
        return remote(
            piece, piece, kv_send.at[kind, side, step, half], kv_recv.at[kind, side, step, half],
            at_z(z_side[side]),
        )

    def kv3(kind, side, owner, count):
        piece = (kb, vb)[kind].at[owner, pl.ds(side * count, count)]
        return remote(
            piece, piece, kv_send.at[kind, side, 3, 0], kv_recv.at[kind, side, 3, 0], at_z(z_side[side])
        )

    def turn(at):
        step = lax.div(at + 1, 2)
        return wrap(jnp.where(lax.rem(at, 2) == 1, z - step, z + step), NZ)

    def wx(side, at):
        piece = wb.at[x, turn(at)]
        return remote(piece, piece, wx_send.at[side, at], wx_recv.at[side, at], at_x(x_side[side]))

    def wx_arrived(side, at):
        piece = wb.at[x_side[1 - side], turn(at)]
        remote(piece, piece, wx_send.at[side, at], wx_recv.at[side, at], at_x(x_side[side])).wait_recv()

    def wy_rows(side):
        return pl.ds(0, CUT) if side == RIGHT else pl.ds(CUT, WCOLS - CUT)

    def wy(side, at):
        piece = wb.at[x_side[1 - side], turn(at), wy_rows(side)]
        return remote(piece, piece, wy_send.at[side, at], wy_recv.at[side, at], at_x(x_side[side]))

    def wy_arrived(side, at):
        piece = wb.at[wrap(x + 2, NX), turn(at), wy_rows(side)]
        remote(piece, piece, wy_send.at[side, at], wy_recv.at[side, at], at_x(x_side[side])).wait_recv()

    def spread(at):
        for side in (RIGHT, LEFT):
            wx(side, at).start()

    def hand_on(at):
        for side in (RIGHT, LEFT):
            wx_arrived(side, at)
            wy(side, at).start()

    for kind in (0, 1):
        for step in (1, 3, 2):
            @pl.when(wants(wrap(x + step, NX), x))
            def _():
                first(kind, step).start()
    own[0].wait()
    for side in (RIGHT, LEFT):
        wz(side, 0).start()
    for kind in (0, 1):
        own[1 + kind].wait()
        for side in (RIGHT, LEFT):
            kv0(kind, side, jnp.int32(0)).start()
    for step in (1, 3, 2):
        first(2, step).start()
    spread(jnp.int32(0))

    rows_at = lax.broadcasted_iota(jnp.int32, (128, 128), 0)
    lanes_at = lax.broadcasted_iota(jnp.int32, (128, 128), 1)
    zero = jnp.zeros((128, 128), jnp.float32)
    slot_row = jnp.broadcast_to(slot_ref[...].astype(jnp.float32), (128, 128))
    doc_row = jnp.broadcast_to(doc_ref[...].astype(jnp.float32), (128, 128))
    clip = jnp.sum(jnp.where(rows_at == lanes_at, slot_row, zero), axis=1, keepdims=True)
    clip = jnp.broadcast_to(clip, (128, 128))
    doc = jnp.sum(jnp.where(clip == lanes_at.astype(jnp.float32), doc_row, zero), axis=1, keepdims=True)
    doc = jnp.broadcast_to(doc, (128, 128))
    start = jnp.sum(jnp.where(doc_row < doc, zero + 1.0, zero), axis=1, keepdims=True)
    start = jnp.broadcast_to(start, (128, 128))
    spans = ROWS // SPAN
    wanted = (lax.div(lanes_at, spans) * NZ + z) * spans + lax.rem(lanes_at, spans)
    chosen = rows_at == wanted
    clip_q = jnp.sum(jnp.where(chosen, clip, zero), axis=0, keepdims=True)
    start_q = jnp.sum(jnp.where(chosen, start, zero), axis=0, keepdims=True)
    visible = (clip <= clip_q) & (clip >= start_q)
    seen[...] = jnp.where(visible, zero, zero + MASKED)

    def expand(zz, unused):
        for at in range(NX):
            partner = 2 * lax.div(x, 2) + 1 - lax.rem(x, 2)
            source = wrap(x + (0, -1, 1, 2)[at], NX)
            if at == 1:
                source = jnp.where(full, source, partner)
            for span in range(spans):
                row = seen[pl.ds((source * NZ + zz) * spans + span, 1), :]
                row = jnp.broadcast_to(row, (SPAN, 128)).astype(jnp.bfloat16)
                bias[zz, at, pl.ds(span * SPAN, SPAN), :] = row
        return unused

    lax.fori_loop(0, NZ, expand, 0)
    span_at = lax.div(lax.broadcasted_iota(jnp.int32, (ROWS, 128), 0), SPAN)
    lane_at = lax.broadcasted_iota(jnp.int32, (ROWS, 128), 1)
    for part in range(NX):
        hot[part] = jnp.where(lane_at == span_at + part * spans, 1.0, 0.0).astype(jnp.bfloat16)
    top[...] = jnp.full(top.shape, LOWEST, jnp.float32)
    acc[...] = jnp.zeros(acc.shape, jnp.float32)

    def attend(pairs, parts):
        count = 2 * ROWS

        def join(buf, width):
            return [buf[block, pl.ds(2 * half, 2)].reshape(count, width) for block, half in pairs]

        k_all = jnp.concatenate(
            [jnp.concatenate(both, axis=1) for both in zip(join(kb, HEAD_DIM), join(bias, 128))], axis=0
        )
        ones = jnp.ones((count, 128), jnp.bfloat16)
        v_all = jnp.concatenate([jnp.concatenate([v, ones], axis=1) for v in join(vb, HEAD_DIM)], axis=0)
        count *= len(pairs)
        for part in parts:
            q_all = jnp.concatenate([qb[part], hot[part]], axis=1)
            scores = lax.dot_general(q_all, k_all, NT, preferred_element_type=jnp.float32)
            old = top[part]
            new = jnp.maximum(old, jnp.broadcast_to(jnp.max(scores, axis=1, keepdims=True), old.shape))
            scaled = new * SCALE
            weights = jnp.exp2(scores * SCALE - jnp.concatenate([scaled] * (count // 128), axis=1))
            shrink = jnp.exp2(old * SCALE - scaled)
            fresh = jnp.dot(weights.astype(jnp.bfloat16), v_all, preferred_element_type=jnp.float32)
            acc[part] = acc[part] * jnp.concatenate([shrink, shrink], axis=1) + fresh
            top[part] = new

    def w_step(step):
        for side in (RIGHT, LEFT):
            wz_arrived(side, step)
            wz(side, step + 1).start()
        spread(jnp.int32(2 * step + 1))
        spread(jnp.int32(2 * step + 2))

    def tiles_from(step):
        by = wrap(x - step, NX)

        @pl.when(wants(x, by))
        def _():
            for kind in (0, 1):
                first_arrived(kind, step)
                for side in (RIGHT, LEFT):
                    kv0(kind, side, place(x, step)).start()

    w_step(0)
    tiles_from(1)
    tiles_from(3)
    w_step(1)
    tiles_from(2)
    for step in (1, 3, 2):
        first_arrived(2, step)
    own[3].wait()

    per = jnp.where(full, 1, 2)

    def main(index, unused):
        stage = index - lead
        step, half = lax.div(stage + halves, halves) - 1, lax.rem(stage + halves, halves)
        right, left = wrap(z - step - 1, NZ), wrap(z + step + 1, NZ)

        @pl.when(stage >= 0)
        def _():
            for kind in (0, 1):
                for side, owner in ((RIGHT, right), (LEFT, left)):
                    kv(kind, side, step, half, owner).wait_recv()

                    @pl.when(step < 2)
                    def _():
                        kv(kind, side, step + 1, half, owner).start()

                    @pl.when((step == 2) & full & (half == side))
                    def _():
                        kv3(kind, side, owner, 2).start()

                    @pl.when((step == 2) & not_full)
                    def _():
                        kv3(kind, side, owner, 1).start()

        is_own = stage < 0
        attend(
            (
                (jnp.where(is_own, z, right), jnp.where(is_own, 0, half)),
                (jnp.where(is_own, z, left), jnp.where(is_own, 1, half)),
            ),
            range(NX),
        )

        @pl.when(stage == 0)
        def _():
            w_step(2)

        @pl.when(stage == 1)
        def _():
            for side in (RIGHT, LEFT):
                wz_arrived(side, 3)
            spread(jnp.int32(7))

        def hand(at, unused):
            hand_on(at)
            return unused

        begun = jnp.minimum(per * jnp.maximum(stage - 1, 0), EARLY)
        lax.fori_loop(begun, jnp.minimum(per * jnp.maximum(stage, 0), EARLY), hand, 0)
        return unused

    lax.fori_loop(0, lead + 3 * halves, main, 0)

    def answer(part):
        return remote(ost.at[part], ob.at[x], o_send.at[part], o_recv.at[x], at_x(part))

    def answer_stat(part):
        return remote(
            stat_out.at[part], stat_in.at[x], stat_send.at[part], stat_recv.at[x], at_x(part)
        )

    eye = rows_at == lanes_at

    def finish(part):
        total = acc[part]
        result = (total[:, :HEAD_DIM] / total[:, HEAD_DIM:]).astype(jnp.bfloat16)
        ost[part] = result

        @pl.when(part != x)
        def _():
            answer(part).start()

        @pl.when(part == x)
        def _():
            ob[x] = result

        @pl.when(not_full)
        def _():
            scaled = top[part] * SCALE
            sums = total[:, HEAD_DIM:]
            rows = []
            for which in (scaled, sums):
                for at in (0, 128):
                    rows.append(jnp.sum(jnp.where(eye, which[at:at + 128], zero), axis=0, keepdims=True))
            stats = jnp.concatenate(rows + [zero[:4]], axis=0)
            stat_out[part] = stats

            @pl.when(part != x)
            def _():
                answer_stat(part).start()

            @pl.when(part == x)
            def _():
                stat_in[x] = stats

    last = wrap(z + NZ // 2, NZ)

    def arrive_last(count):
        for kind in (0, 1):
            for side in (RIGHT, LEFT):
                kv3(kind, side, last, count).wait_recv()

    @pl.when(full)
    def _():
        arrive_last(2)

    @pl.when(not_full)
    def _():
        arrive_last(1)

    attend(((jnp.where(full, last, z), 0), (last, jnp.where(full, 1, 0))), range(NX))
    for part in range(NX):
        finish(part)

    for at in range(EARLY, NZ):
        hand_on(jnp.int32(at))


    for giver in range(NX):
        @pl.when(giver != x)
        def _():
            remote(ost.at[0], ob.at[giver], o_send.at[0], o_recv.at[giver], at_x(x_side[0])).wait_recv()

            @pl.when(jnp.logical_not(is_full(giver)))
            def _():
                remote(
                    stat_out.at[0], stat_in.at[giver], stat_send.at[0], stat_recv.at[giver], at_x(x_side[0])
                ).wait_recv()

    def column(stats, first_row):
        parts = []
        for at in (first_row, first_row + 1):
            row = jnp.broadcast_to(stats[at:at + 1], (128, 128))
            whole = jnp.sum(jnp.where(eye, row, zero), axis=1, keepdims=True)
            parts.append(jnp.broadcast_to(whole, (128, 128)))
        return jnp.concatenate(parts, axis=0)

    one, two = 1 - core, 2 + core
    top_one, top_two = column(stat_in[one], 0), column(stat_in[two], 0)
    best = jnp.maximum(top_one, top_two)
    share_one = column(stat_in[one], 2) * jnp.exp2(top_one - best)
    share_two = column(stat_in[two], 2) * jnp.exp2(top_two - best)
    middle = ob[one].astype(jnp.float32) * share_one + ob[two].astype(jnp.float32) * share_two
    middle = (middle / (share_one + share_two)).astype(jnp.bfloat16)
    attn = jnp.concatenate([ob[core], middle, ob[NX - 1 - core]], axis=1)

    pieces = (x, x_side[0], x_side[1], wrap(x + 2, NX))
    owners = [wrap(y + away, NY) for away in (4, 3, -3, 2, -2, 1, -1, 0)]
    cuts = ((0, 1), (1, 2), (3, 5))

    def to_sibling(piece, cut):
        rows = pl.ds(*cuts[cut])
        return remote(
            sib_out.at[piece, rows], sib_in.at[piece, rows],
            sib_send.at[piece, cut], sib_recv.at[piece, cut], sibling,
        )

    def rs(side, step, piece):
        return remote(
            rs_out.at[side, step, piece], rs_in.at[side, step, piece],
            rs_send.at[side, step, piece], rs_recv.at[side, step, piece], at_y(y_side[side]),
        )

    def here(piece, rank):
        return prod[piece, owners[rank], core] + sib_in[piece, rank].astype(jnp.float32)

    def travels(side, step, piece):
        return step > 0 or piece % 2 == side

    def pass_on(side, step, piece):
        total = here(piece, 2 * step - 1 + side if step else 0)
        if step > 0 and travels(side, step - 1, piece):
            rs(side, step - 1, piece).wait_recv()
            total = total + rs_in[side, step - 1, piece].astype(jnp.float32)
        rs_out[side, step, piece] = total.astype(jnp.bfloat16)
        rs(side, step, piece).start()

    def begin(piece):
        to_sibling(piece, 0).wait_recv()
        pass_on(piece % 2, 0, piece)
        to_sibling(piece, 1).wait_recv()
        pass_on(1 - piece % 2, 1, piece)

    for piece in range(NX):
        if piece == NX - 1:
            begin(NX - 2)
            for side in (RIGHT, LEFT):
                for at in range(NZ):
                    wy_arrived(side, jnp.int32(at))
        part = lax.dot_general(
            attn, wb[pieces[piece]].reshape(PIECE, WROWS), NT, preferred_element_type=jnp.float32
        )
        prod[piece] = part.reshape(NY, 2, MINE, PIECE)
        for rank in range(NY):
            sib_out[piece, rank] = prod[piece, owners[rank], 1 - core].astype(jnp.bfloat16)
            if rank in (0, 2):
                to_sibling(piece, rank // 2).start()
        if piece in (1, 2):
            begin(piece - 1)
    for piece in range(NX):
        to_sibling(piece, 2).start()
    begin(NX - 1)
    late = ((1, 3, 0, 2), (0, 2, 1, 3))
    for at in (2, 3):
        for side in (RIGHT, LEFT):
            pass_on(side, 1, late[side][at])
    for piece in range(NX):
        to_sibling(piece, 2).wait_recv()
    for step in range(2, NY // 2):
        for at in range(NX):
            for side in (RIGHT, LEFT):
                pass_on(side, step, late[side][at])
    for step in (1, 2, 3):
        first(2, step).wait_send()

        @pl.when(wants(wrap(x + step, NX), x))
        def _():
            for kind in (0, 1):
                first(kind, step).wait_send()

    def sent(half, unused):
        for kind in (0, 1):
            for side in (RIGHT, LEFT):
                for step in (0, 1, 2):
                    kv(kind, side, step, half, z).wait_send()
        return unused

    lax.fori_loop(0, halves, sent, 0)
    for kind in (0, 1):
        for side in (RIGHT, LEFT):
            @pl.when(full)
            def _():
                kv3(kind, side, z, 2).wait_send()

            @pl.when(not_full)
            def _():
                kv3(kind, side, z, 1).wait_send()
    for side in (RIGHT, LEFT):
        for step in range(NZ // 2):
            wz(side, step).wait_send()
        for at in range(NZ):
            wx(side, jnp.int32(at)).wait_send()
            wy(side, jnp.int32(at)).wait_send()
    for part in range(NX):
        @pl.when(part != x)
        def _():
            answer(part).wait_send()

            @pl.when(not_full)
            def _():
                answer_stat(part).wait_send()
    for piece in range(NX):
        for cut in range(3):
            to_sibling(piece, cut).wait_send()
    for step in range(NY // 2 - 1):
        for piece in range(NX):
            for side in (RIGHT, LEFT):
                if travels(side, step, piece):
                    rs(side, step, piece).wait_send()

    for piece in (1, 0, 3, 2):
        total = here(piece, NY - 1)
        for side in (RIGHT, LEFT):
            rs(side, NY // 2 - 1, piece).wait_recv()
            total = total + rs_in[side, NY // 2 - 1, piece].astype(jnp.float32)
        out_ref[:, pl.ds(pl.multiple_of(pieces[piece] * PIECE, PIECE), PIECE)] = total.astype(jnp.bfloat16)
    for piece in range(NX):
        for side in (RIGHT, LEFT):
            rs(side, NY // 2 - 1, piece).wait_send()


def local(query, keys, values, span_slot, span_doc, w_out):
    whole = pl.BlockSpec(memory_space=pltpu.VMEM)
    remote = pl.BlockSpec(memory_space=pl.ANY)
    bf16, f32 = jnp.bfloat16, jnp.float32
    dma = pltpu.SemaphoreType.DMA
    return pl.pallas_call(
        kernel,
        out_shape=jax.ShapeDtypeStruct((MINE, D), bf16),
        in_specs=[remote] * 4 + [whole] * 2,
        out_specs=whole,
        scratch_shapes=[
            pltpu.VMEM((NX, ROWS, HEAD_DIM), bf16),
            pltpu.VMEM((NX, ROWS, 128), bf16),
            pltpu.VMEM((NZ, NX, ROWS, HEAD_DIM), bf16),
            pltpu.VMEM((NZ, NX, ROWS, HEAD_DIM), bf16),
            pltpu.VMEM((128, 128), f32),
            pltpu.VMEM((NZ, NX, ROWS, 128), bf16),
            pltpu.VMEM((NX, NZ, WCOLS, WROWS), bf16),
            pltpu.VMEM((NX, ROWS, 128), f32),
            pltpu.VMEM((NX, ROWS, 256), f32),
            pltpu.VMEM((NX, ROWS, HEAD_DIM), bf16),
            pltpu.VMEM((NX, ROWS, HEAD_DIM), bf16),
            pltpu.VMEM((NX, 8, 128), f32),
            pltpu.VMEM((NX, 8, 128), f32),
            pltpu.VMEM((NX, NY, 2, MINE, PIECE), f32),
            pltpu.VMEM((NX, NY, MINE, PIECE), bf16),
            pltpu.VMEM((NX, NY, MINE, PIECE), bf16),
            pltpu.VMEM((2, NY // 2, NX, MINE, PIECE), bf16),
            pltpu.VMEM((2, NY // 2, NX, MINE, PIECE), bf16),
            dma((4,)),
            dma((3, 3)), dma((3, 3)),
            dma((2, 2, 4, 2)), dma((2, 2, 4, 2)),
            dma((2, NZ // 2)), dma((2, NZ // 2)),
            dma((2, NZ)), dma((2, NZ)),
            dma((2, NZ)), dma((2, NZ)),
            dma((NX,)), dma((NX,)),
            dma((NX,)), dma((NX,)),
            dma((NX, 3)), dma((NX, 3)),
            dma((2, NY // 2, NX)), dma((2, NY // 2, NX)),
        ],
        compiler_params=pltpu.CompilerParams(
            collective_id=0, has_side_effects=True, vmem_limit_bytes=56 << 20
        ),
        cost_estimate=pl.CostEstimate(
            flops=2 * BLOCK * 8192 * 512 + 2 * ROWS * WROWS * D,
            bytes_accessed=1 << 21, transcendentals=BLOCK * 8192,
        ),
    )(query, keys, values, w_out.T, span_slot.reshape(1, 128), span_doc.reshape(1, 128))


def solution(mesh):
    placed = (P("ctx", "head"), P("ctx", "head"), P("ctx", "head"), P(), P(), P("head", "ctx"))
    return jax.shard_map(
        local, mesh=mesh, in_specs=placed, out_specs=P(("ctx", "head"), None), check_vma=False
    )
```
